128 devices in a mesh: list: 16 (over y, z), expert: 8 (over x, core).
Axes of the slice: x: 4, y: 4, z: 4, core: 2. Of those that a mesh axis runs over, the one named last changes fastest.
Arguments:
- hidden: bfloat16 [16384, 4096], P(('list', 'expert')), may hold values from -100 to 100
- query: bfloat16 [16384, 4096], P('list', 'expert'), may hold values from -32 to 32
- candidate_key_value: bfloat16 [16384, 2, 256], P('list'), may hold values from -6 to 6
- prefix_key_value: bfloat16 [1536, 2, 256], P('list'), may hold values from -36 to 36
- segment_ids: int32 [16, 1024], P('list'), may hold values from 0 to 15, never falling along the last dimension, each value on 1 to 128 neighbouring positions
- o_weight: bfloat16 [4096, 4096], P('expert', 'list'), may hold values from -3 to 3
- norm_gain: bfloat16 [4096], replicated, may hold values from 0.099609375 to 1.8984375
- routes: int32 [16384, 2], P(('list', 'expert')), may hold values from 0 to 63, all different within a row; in each aligned block of 128 rows (0 to 127, 128 to 255, ...) at most 8 rows name the same one
- route_weights: float32 [16384, 2], P(('list', 'expert')), may hold values from 0.1 to 1
- w_gate: bfloat16 [128, 4096, 768], P(('list', 'expert')), may hold values from -0.09375 to 0.09375
- w_up: bfloat16 [128, 4096, 768], P(('list', 'expert')), may hold values from -0.09375 to 0.09375
- w_down: bfloat16 [128, 768, 4096], P(('list', 'expert')), may hold values from -0.15625 to 0.15625
Outputs:
- attended: bfloat16 [16384, 4096], P(('list', 'expert'))
- moe_out: bfloat16 [16384, 4096], P(('list', 'expert'))
The draws below stay inside these ranges and needn't reach their ends.
Inputs may be any that keep to these rules, and one draw needn't show every extreme that they name: `segment_ids`: each row numbers the 16 candidates of one list in order. `routes`: among the 128 tokens of one device no expert is named more than 8 times, and in every draw some expert is named exactly 8 times by the tokens of some device.
All inputs are finite; a program needn't handle non-finite values.
Results may differ from the reference program's by a relative error of at most 0.03.
Values may be sent and summed in bfloat16 or wider, within the bound.
No kernel may reach another device: no remote copies, remote signals or barrier semaphores. Data moves between devices by JAX's collectives and lax.ppermute only.
A program may use at most 192 MiB of HBM per device.

```python
import math
import jax
import jax.numpy as jnp
import numpy as np
from jax import lax

D = 4096
QUERY_HEADS = 32
KEY_VALUE_HEADS = 2
HEAD_SIZE = 128
FF = 1536
TOP = 2
TOK_DEV = 128
HALF = 768
EXPERTS = 64
CAP = 8
LIST_TOKENS = 1024
NCAND = 16
CAND_MOST = 128
PREFIX_LENGTH = 1536
TOKEN_COUNT = 16384
N_LIST = 16
N_EXPERT = 8
DEVICES = 128


def draw_hidden(key, part):
    complete_shape = (TOKEN_COUNT, D)
    col_scale = jnp.exp(jax.random.uniform(jax.random.fold_in(key, 3), (1, D), jnp.float32, math.log(0.4), math.log(4.0)))
    base_draw = jnp.clip(jax.random.normal(jax.random.fold_in(key, 1), complete_shape, jnp.float32), -4.0, 4.0)
    row_scale = jnp.exp(jax.random.uniform(jax.random.fold_in(key, 2), (TOKEN_COUNT, 1), jnp.float32, math.log(0.3), math.log(3.0)))
    return (base_draw * row_scale * col_scale).astype(jnp.bfloat16)


def draw_query(key, part):
    complete_shape = (TOKEN_COUNT, QUERY_HEADS * HEAD_SIZE)
    result = jnp.clip(jax.random.normal(jax.random.fold_in(key, 11), complete_shape, jnp.float32), -4.0, 4.0)
    return result.astype(jnp.bfloat16)


def draw_prefix_key_value(key, part):
    complete_shape = (PREFIX_LENGTH, 2, KEY_VALUE_HEADS * HEAD_SIZE)
    result = jnp.clip(jax.random.normal(jax.random.fold_in(key, 21), complete_shape, jnp.float32), -4.0, 4.0)
    return result.astype(jnp.bfloat16)


def steps_of(rng, shape, cuts, least, high):
    factor_of = 1.0
    for dim, blocks in cuts:
        steps = jax.random.uniform(jax.random.fold_in(jax.random.fold_in(rng, 6), dim), (blocks,), jnp.float32, least / len(cuts), high / len(cuts))
        factor_of = factor_of * jnp.repeat(jnp.exp(steps), shape[dim] // blocks).reshape((-1,) + (1,) * (len(shape) - 1 - dim))
    return factor_of


def profile(number_of, total, bound, skew):
    weights = [(1 << 20) // math.isqrt(rank ** skew) + 1 for rank in range(2, number_of + 1)]
    rest, given = total - bound - (number_of - 1), [1] * (number_of - 1)
    while rest > 0:
        movable = [i for i in range(number_of - 1) if given[i] < bound]
        mass, left = sum([weights[i] for i in movable]), rest
        for i in movable:
            more = min(bound - given[i], max(1, left * weights[i] // mass), rest)
            given[i] = given[i] + more
            rest = rest - more
    return np.array([bound] + given)


def uneven_parts(own_key, number_of, total, reach, lean):
    if number_of == 2:
        one = jax.random.randint(own_key, (), max(1, total - reach), min(reach, total - 1) + 1)
        return jnp.stack([one, total - one])
    tallies = jnp.asarray(profile(number_of, total, reach, lean), jnp.int32)
    twos = (number_of - 1) // 2
    giver, taker = tallies[1:1 + 2 * twos:2], tallies[2:2 + 2 * twos:2]
    slack = jnp.minimum(giver - 1, reach - taker)
    moved = jax.random.randint(jax.random.fold_in(own_key, 1), (twos,), 0, 1 << 20) % (slack + 1)
    tallies = tallies.at[1:1 + 2 * twos:2].set(giver - moved).at[2:2 + 2 * twos:2].set(taker + moved)
    return tallies[jax.random.permutation(jax.random.fold_in(own_key, 2), number_of)]


def assign_block(key, own, number, rows, amount, top, limit, lean):
    ranking = jax.random.permutation(key, amount)
    heavy_load, ordinary = load_shares(amount, rows * top, limit, lean, True), load_shares(amount, rows * top, limit, lean, False)
    places = jnp.arange(amount)

    def named(sizes, rotation):
        used = int((sizes > 0).sum())
        fixed = max(1, used // 4)
        passed = fixed + (places - fixed + rotation * (used - fixed)) % max(1, amount - fixed)
        return jnp.zeros((amount,), jnp.int32).at[ranking[jnp.where(places < fixed, places, passed)]].set(jnp.asarray(sizes, jnp.int32))

    sizes = jnp.where(number % 4 == 0, named(heavy_load, number // 4), named(ordinary, number - number // 4 - 1))
    mixed = jax.random.permutation(jax.random.fold_in(own, 3), amount)
    donor, sink = mixed[0:amount // 2 * 2:2], mixed[1:amount // 2 * 2:2]
    slack = jnp.minimum(sizes[donor] - 1, limit - sizes[sink]) // 2
    slack = jnp.where((donor == ranking[0]) | (sink == ranking[0]) | (sizes[sink] == 0), 0, jnp.maximum(slack, 0))
    passed = jax.random.randint(jax.random.fold_in(own, 4), (amount // 2,), 0, 1 << 20) % (slack + 1)
    sizes = sizes.at[donor].add(-passed).at[sink].add(passed)
    members = jnp.searchsorted(jnp.cumsum(sizes), jnp.arange(rows * top), side="right").astype(jnp.int32)
    table = members.reshape(top, rows).T
    table = table[jax.random.permutation(jax.random.fold_in(own, 1), rows)]
    rotation = jax.random.randint(jax.random.fold_in(own, 2), (rows, 1), 0, top)
    return jnp.take_along_axis(table, (jnp.arange(top)[None, :] + rotation) % top, axis=1)


def load_shares(amount, total, reach, slope, full):
    weights = [(1 << 20) // math.isqrt(standing ** slope) + 1 for standing in range(1, amount + 1)]
    largest = reach if full else min(reach, max(-(-total // amount), total * weights[0] // sum(weights)))
    least = 1 if total - largest >= amount - 1 else 0
    given, rest = [largest] + [least] * (amount - 1), total - largest - least * (amount - 1)
    while rest > 0:
        free = [i for i in range(1, amount) if given[i] < largest] or [i for i in range(1, amount) if given[i] < reach]
        pool, left = sum([weights[i] for i in free]), rest
        for i in free:
            more = min(reach - given[i], max(1, left * weights[i] // pool), rest)
            given[i] = given[i] + more
            rest = rest - more
    return np.array(given)


def noise(own_key, dims, width, most, shards=(), kind=jnp.bfloat16):
    factor_of = steps_of(own_key, dims, shards, -0.22, 0.18) if shards else 1.0
    drawn = jax.random.normal(own_key, dims, jnp.float32) * width * factor_of
    return jnp.minimum(jnp.maximum(drawn, -most), most).astype(kind)


def setup_inputs(seed: int = 0) -> dict:
    splits = jax.random.split(jax.random.key(seed), 13)
    hidden = draw_hidden(jax.random.fold_in(splits[12], 71), 0)
    query = draw_query(jax.random.fold_in(splits[12], 71), 0)
    candidate_key_value = noise(splits[2], (TOKEN_COUNT, 2, KEY_VALUE_HEADS * HEAD_SIZE), 1.0, 6.0, ((0, 16),))
    prefix_key_value = draw_prefix_key_value(jax.random.fold_in(splits[12], 71), 0)
    segment_ids = jax.vmap(lambda own: jnp.searchsorted(jnp.cumsum(uneven_parts(own, NCAND, LIST_TOKENS, CAND_MOST, 2)), jnp.arange(LIST_TOKENS), side="right"))(jax.random.split(splits[4], N_LIST)).reshape((N_LIST, LIST_TOKENS)).astype(jnp.int32)
    o_weight = noise(splits[5], (QUERY_HEADS * HEAD_SIZE, D), 0.5, 3.0, ((0, 8), (1, 16)))
    norm_gain = jnp.clip(1.0 + 0.18 * jax.random.normal(splits[6], (D,), jnp.float32), 0.099609375, 1.8984375).astype(jnp.bfloat16)
    routes_keys = jax.random.split(jax.random.fold_in(splits[7], 1), TOKEN_COUNT // TOK_DEV)
    routes_turns = jax.random.permutation(jax.random.fold_in(splits[7], 3), TOKEN_COUNT // TOK_DEV)
    routes = jax.vmap(lambda own, number: assign_block(jax.random.fold_in(splits[7], 2), own, number, TOK_DEV, EXPERTS, TOP, CAP, 2))(routes_keys, routes_turns).reshape((TOKEN_COUNT, TOP))
    route_weights = jnp.clip(jnp.exp(math.log(1.0) - 2.3025851 * jax.random.uniform(splits[8], (TOKEN_COUNT, TOP), jnp.float32) ** steps_of(splits[8], (TOKEN_COUNT, TOP), ((0, 128),), -0.2, 0.2)), 0.1, 1.0)
    w_gate = noise(splits[9], (2 * EXPERTS, D, HALF), D ** -0.5, 0.09375, ((0, 128),))
    w_up = noise(splits[10], (2 * EXPERTS, D, HALF), D ** -0.5, 0.09375, ((0, 128),))
    w_down = noise(splits[11], (2 * EXPERTS, HALF, D), FF ** -0.5, 0.15625, ((0, 128),))
    return dict(hidden=hidden, query=query, candidate_key_value=candidate_key_value, prefix_key_value=prefix_key_value, segment_ids=segment_ids, o_weight=o_weight, norm_gain=norm_gain, routes=routes, route_weights=route_weights, w_gate=w_gate, w_up=w_up, w_down=w_down)


def reference(hidden, query, candidate_key_value, prefix_key_value, segment_ids, o_weight, norm_gain, routes, route_weights, w_gate, w_up, w_down):
    group_width = QUERY_HEADS // KEY_VALUE_HEADS
    per_group = QUERY_HEADS // N_EXPERT
    scale = 1.0 / math.sqrt(HEAD_SIZE)
    q_lists = query.reshape(N_LIST, LIST_TOKENS, QUERY_HEADS, HEAD_SIZE)
    key_value_lists = candidate_key_value.reshape(N_LIST, LIST_TOKENS, 2, KEY_VALUE_HEADS, HEAD_SIZE)
    prefix_head_rows = prefix_key_value.reshape(PREFIX_LENGTH, 2, KEY_VALUE_HEADS, HEAD_SIZE)
    wo_groups = o_weight.reshape(N_EXPERT, per_group * HEAD_SIZE, D)
    position = jnp.arange(LIST_TOKENS).astype(jnp.int32)

    def one_list(inputs):
        q_list, kv_list, segment = inputs
        allowed = (segment[:, None] == segment[None, :]) & (position[None, :] <= position[:, None])
        key_mask = jnp.concatenate([jnp.ones((LIST_TOKENS, PREFIX_LENGTH), dtype=bool), allowed], axis=1)

        def one_head(head):
            key_value_index = head // group_width
            q_head = lax.dynamic_index_in_dim(q_list, head, 1, keepdims=False)
            key_rows = jnp.concatenate([lax.dynamic_index_in_dim(prefix_head_rows[:, 0], key_value_index, 1, keepdims=False), lax.dynamic_index_in_dim(kv_list[:, 0], key_value_index, 1, keepdims=False)], axis=0)
            value_rows = jnp.concatenate([lax.dynamic_index_in_dim(prefix_head_rows[:, 1], key_value_index, 1, keepdims=False), lax.dynamic_index_in_dim(kv_list[:, 1], key_value_index, 1, keepdims=False)], axis=0)
            scores = jnp.dot(q_head, key_rows.T, preferred_element_type=jnp.float32) * scale
            scores = jnp.where(key_mask, scores, jnp.float32(-1e+30))
            row_max = lax.optimization_barrier(jnp.max(scores, axis=-1, keepdims=True))
            expo = jnp.exp(scores - row_max)
            total = lax.optimization_barrier(jnp.sum(expo, axis=-1, keepdims=True))
            summed = jnp.dot(expo.astype(jnp.bfloat16), value_rows, preferred_element_type=jnp.float32)
            return (summed / total).astype(jnp.bfloat16)
        head_outs = lax.map(one_head, jnp.arange(QUERY_HEADS).astype(jnp.int32))
        merged = jnp.transpose(head_outs, (1, 0, 2)).reshape(LIST_TOKENS, N_EXPERT, per_group * HEAD_SIZE)

        def one_group(index):
            block = lax.dynamic_index_in_dim(merged, index, 1, keepdims=False)
            weight_rows = lax.dynamic_index_in_dim(wo_groups, index, 0, keepdims=False)
            rounded = lax.optimization_barrier(jnp.dot(block, weight_rows, preferred_element_type=jnp.float32).astype(jnp.bfloat16))
            return rounded.astype(jnp.float32)
        return lax.optimization_barrier(jnp.sum(lax.map(one_group, jnp.arange(N_EXPERT).astype(jnp.int32)), axis=0))
    attn = lax.map(one_list, (q_lists, key_value_lists, segment_ids)).reshape(TOKEN_COUNT, D)
    attended = (hidden.astype(jnp.float32) + attn).astype(jnp.bfloat16)
    widened = attended.astype(jnp.float32)
    mean_square = lax.optimization_barrier(jnp.mean(widened * widened, axis=-1, keepdims=True))
    normed = (widened * lax.rsqrt(mean_square + 1e-06) * norm_gain.astype(jnp.float32)).astype(jnp.bfloat16)
    block_routes = routes.reshape(DEVICES, TOK_DEV * TOP)
    block_weights = route_weights.reshape(DEVICES, TOK_DEV * TOP)
    pair_pos = jnp.arange(TOK_DEV * TOP).astype(jnp.int32)
    slot_ids = jnp.arange(CAP).astype(jnp.int32)
    block_base = (jnp.arange(DEVICES).astype(jnp.int32) * TOK_DEV)[:, None]

    def one_expert(running, expert):
        matched = (block_routes == expert).astype(jnp.int32)
        ranked = jnp.cumsum(matched, axis=1) - matched
        picked = ((matched[:, :, None] == 1) & (ranked[:, :, None] == slot_ids[None, None, :])).astype(jnp.int32)
        pair_index = lax.optimization_barrier(jnp.sum(picked * pair_pos[None, :, None], axis=1))
        token_index = (block_base + pair_index // TOP).reshape(-1).astype(jnp.int32)
        slot_weight = lax.optimization_barrier(jnp.sum(picked.astype(jnp.float32) * block_weights[:, :, None], axis=1)).reshape(-1)
        expert_rows = normed[token_index]
        combined = jnp.zeros((DEVICES * CAP, D), jnp.float32)
        for half_index in range(2):
            slab = 2 * expert + half_index
            gate_w = lax.dynamic_index_in_dim(w_gate, slab, 0, keepdims=False)
            up_w = lax.dynamic_index_in_dim(w_up, slab, 0, keepdims=False)
            down_w = lax.dynamic_index_in_dim(w_down, slab, 0, keepdims=False)
            gated = jnp.dot(expert_rows, gate_w, preferred_element_type=jnp.float32)
            upward = jnp.dot(expert_rows, up_w, preferred_element_type=jnp.float32)
            activ = (jax.nn.silu(gated) * upward).astype(jnp.bfloat16)
            rounded = lax.optimization_barrier(jnp.dot(activ, down_w, preferred_element_type=jnp.float32).astype(jnp.bfloat16))
            combined = combined + rounded.astype(jnp.float32)
        running = running.at[token_index].add(slot_weight[:, None] * combined)
        return (running, None)
    start_total = jnp.zeros((TOKEN_COUNT, D), jnp.float32)
    total_out, unused = lax.scan(one_expert, start_total, jnp.arange(EXPERTS).astype(jnp.int32))
    moe_out = total_out.astype(jnp.bfloat16)
    return (attended, moe_out)
```

```python
import math

import jax
import jax.numpy as jnp
from jax import lax
from jax.experimental import pallas as pl
from jax.experimental.pallas import tpu as pltpu
from jax.sharding import Mesh
from jax.sharding import PartitionSpec as P

D = 4096
QUERY_HEADS = 32
KEY_VALUE_HEADS = 2
HEAD_SIZE = 128
TOP = 2
BLOCK = 128
CAP = 8

LIST = ("y", "z")
EXPERT = ("x", "core")
CHIP = ("y", "z", "x")
ALL = ("y", "z", "x", "core")
SWAP = [(0, 1), (1, 0)]

masked_score = -1e30
MIB = 1 << 20


def attention_kernel(q_ref, prefix_ref, cand_ref, segment_col_ref, segment_row_ref, out_ref):
    block = pl.program_id(0)
    heads = q_ref.shape[1] // HEAD_SIZE
    factor = math.log2(math.e) / math.sqrt(HEAD_SIZE)
    start = pl.multiple_of(jnp.maximum(block - 1, 0) * BLOCK, BLOCK)
    window = cand_ref[pl.ds(start, 2 * BLOCK), :]
    query_at = block * BLOCK + lax.broadcasted_iota(jnp.int32, (BLOCK, 2 * BLOCK), 0)
    key_at = start + lax.broadcasted_iota(jnp.int32, (BLOCK, 2 * BLOCK), 1)
    key_segment = segment_row_ref[:, pl.ds(start, 2 * BLOCK)]
    allowed = (segment_col_ref[...] == key_segment) & (key_at <= query_at)
    prefix = prefix_ref[...]

    def with_ones(value):
        return jnp.concatenate([value, jnp.ones_like(value)], axis=1)

    prefix_key, prefix_value = prefix[:, :HEAD_SIZE], with_ones(prefix[:, HEAD_SIZE:])
    window_key, window_value = window[:, :HEAD_SIZE], with_ones(window[:, HEAD_SIZE:])
    contract = (((1,), (1,)), ((), ()))
    for head in range(heads):
        columns = slice(head * HEAD_SIZE, (head + 1) * HEAD_SIZE)
        q = q_ref[:, columns]
        far = lax.dot_general(q, prefix_key, contract, preferred_element_type=jnp.float32)
        near = lax.dot_general(q, window_key, contract, preferred_element_type=jnp.float32)
        near = jnp.where(allowed, near, masked_score)
        top = jnp.maximum(
            jnp.max(far, axis=-1, keepdims=True), jnp.max(near, axis=-1, keepdims=True)
        )
        far = jnp.exp2((far - top) * factor).astype(jnp.bfloat16)
        near = jnp.exp2((near - top) * factor).astype(jnp.bfloat16)
        total = jnp.dot(far, prefix_value, preferred_element_type=jnp.float32) + jnp.dot(
            near, window_value, preferred_element_type=jnp.float32
        )
        out_ref[:, columns] = (total[:, :HEAD_SIZE] / total[:, HEAD_SIZE:]).astype(jnp.bfloat16)


def attention(query, prefix, cand, segment):
    tokens, width = query.shape
    return pl.pallas_call(
        attention_kernel,
        out_shape=jax.ShapeDtypeStruct((tokens, width), jnp.bfloat16),
        grid=(tokens // BLOCK,),
        in_specs=[
            pl.BlockSpec((BLOCK, width), lambda i: (i, 0)),
            pl.BlockSpec(prefix.shape, lambda i: (0, 0)),
            pl.BlockSpec(cand.shape, lambda i: (0, 0)),
            pl.BlockSpec((BLOCK, 1), lambda i: (i, 0)),
            pl.BlockSpec((1, tokens), lambda i: (0, 0)),
        ],
        out_specs=pl.BlockSpec((BLOCK, width), lambda i: (i, 0)),
        compiler_params=pltpu.CompilerParams(vmem_limit_bytes=40 * MIB),
        name="attention",
    )(query, prefix, cand, segment.reshape(tokens, 1), segment.reshape(1, tokens))


def norm_pack_kernel(hidden_ref, attn_ref, gain_ref, row_ref, attended_ref, packed_ref):
    attended = (hidden_ref[...].astype(jnp.float32) + attn_ref[...].astype(jnp.float32)).astype(
        jnp.bfloat16
    )
    attended_ref[...] = attended
    widened = attended.astype(jnp.float32)
    mean_square = jnp.mean(widened * widened, axis=-1, keepdims=True)
    normed = (widened * lax.rsqrt(mean_square + 1e-06) * gain_ref[...].astype(jnp.float32)).astype(
        jnp.bfloat16
    )
    rows = packed_ref.shape[0]
    tokens = normed.shape[0]
    at = lax.broadcasted_iota(jnp.int32, (rows, tokens), 0)
    pick = (at == row_ref[0:1, :]) | (at == row_ref[1:2, :])
    pick = pick.astype(jnp.float32).astype(jnp.bfloat16)
    packed_ref[...] = jnp.dot(pick, normed, preferred_element_type=jnp.float32).astype(jnp.bfloat16)


def norm_pack(hidden, attn, gain, rows):
    tokens, width = hidden.shape
    slots = 64 * CAP
    return pl.pallas_call(
        norm_pack_kernel,
        out_shape=(
            jax.ShapeDtypeStruct((tokens, width), jnp.bfloat16),
            jax.ShapeDtypeStruct((slots, width), jnp.bfloat16),
        ),
        compiler_params=pltpu.CompilerParams(vmem_limit_bytes=40 * MIB),
        name="norm_pack",
    )(hidden, attn, gain.reshape(1, width), rows.T)


def combine_kernel(back_ref, row_ref, weight_ref, out_ref):
    tokens, slots = out_ref.shape[0], back_ref.shape[0]
    at = lax.broadcasted_iota(jnp.int32, (tokens, slots), 1)
    back = back_ref[...]
    total = None
    for k in range(TOP):
        pick = (at == row_ref[:, k : k + 1]).astype(jnp.float32).astype(jnp.bfloat16)
        term = weight_ref[:, k : k + 1] * jnp.dot(pick, back, preferred_element_type=jnp.float32)
        total = term if total is None else total + term
    out_ref[...] = total.astype(jnp.bfloat16)


def combine(back, rows, weights):
    slots, width = back.shape
    tokens = rows.shape[0]
    step = 1024
    return pl.pallas_call(
        combine_kernel,
        out_shape=jax.ShapeDtypeStruct((tokens, width), jnp.bfloat16),
        grid=(width // step,),
        in_specs=[
            pl.BlockSpec((slots, step), lambda i: (0, i)),
            pl.BlockSpec((tokens, TOP), lambda i: (0, 0)),
            pl.BlockSpec((tokens, TOP), lambda i: (0, 0)),
        ],
        out_specs=pl.BlockSpec((tokens, step), lambda i: (0, i)),
        compiler_params=pltpu.CompilerParams(vmem_limit_bytes=40 * MIB),
        name="combine",
    )(back, rows, weights)


def half_expert(rows, w_gate, w_up, w_down):
    gated = jnp.dot(rows, w_gate, preferred_element_type=jnp.float32)
    upward = jnp.dot(rows, w_up, preferred_element_type=jnp.float32)
    activ = (jax.nn.silu(gated) * upward).astype(jnp.bfloat16)
    return jnp.dot(activ, w_down, preferred_element_type=jnp.float32)


def slots_of(routes):
    tok_dev = routes.shape[0]
    flat_routes = routes.reshape(-1)
    matched = (flat_routes[:, None] == jnp.arange(64, dtype=jnp.int32)[None, :]).astype(jnp.int32)
    slot_index = jnp.sum((jnp.cumsum(matched, axis=0) - matched) * matched, axis=1)
    return (flat_routes * CAP + slot_index).reshape(tok_dev, TOP)


def local(
    hidden,
    query,
    candidate_key_value,
    prefix_key_value,
    segment_ids,
    o_weight,
    norm_gain,
    routes,
    route_weights,
    w_gate,
    w_up,
    w_down,
):
    heads_dev = query.shape[1] // HEAD_SIZE
    expert_index = lax.axis_index("x") * 2 + lax.axis_index("core")
    head = (expert_index * heads_dev) // (QUERY_HEADS // KEY_VALUE_HEADS)

    def of_head(key_value):
        part = lax.dynamic_slice_in_dim(key_value, head * HEAD_SIZE, HEAD_SIZE, 2)
        return part.reshape(key_value.shape[0], 2 * HEAD_SIZE)

    own_prefix = of_head(prefix_key_value)
    n_list = lax.axis_size(LIST)
    prefix = lax.all_to_all(
        jnp.broadcast_to(own_prefix[None], (n_list,) + own_prefix.shape),
        LIST,
        split_axis=0,
        concat_axis=0,
        tiled=True,
    ).reshape(-1, 2 * HEAD_SIZE)
    wo_full = lax.all_gather(o_weight, LIST, axis=1, tiled=True)
    heads_out = attention(query, prefix, of_head(candidate_key_value), segment_ids[0])
    attn = lax.psum_scatter(
        jnp.dot(heads_out, wo_full, preferred_element_type=jnp.float32).astype(jnp.bfloat16),
        EXPERT,
        scatter_dimension=0,
        tiled=True,
    )
    rows = slots_of(routes)
    attended, packed = norm_pack(hidden, attn, norm_gain, rows)

    def across(slots):
        return lax.all_to_all(
            slots.reshape(64, CAP, D), CHIP, split_axis=0, concat_axis=0, tiled=True
        ).reshape(64 * CAP, D)

    mine = across(packed)
    other = lax.ppermute(mine, "core", SWAP)
    other_part = half_expert(other, w_gate[0], w_up[0], w_down[0]).astype(jnp.bfloat16)
    mine_part = half_expert(mine, w_gate[0], w_up[0], w_down[0])
    both = mine_part + lax.ppermute(other_part, "core", SWAP).astype(jnp.float32)
    back = across(both.astype(jnp.bfloat16))
    return attended, combine(back, rows, route_weights)


def solution(mesh):
    fine = Mesh(mesh.devices.reshape(4, 4, 4, 2), ALL)
    placed = (
        P(ALL, None),
        P(LIST, EXPERT),
        P(LIST, None, None),
        P(LIST, None, None),
        P(LIST, None),
        P(EXPERT, LIST),
        P(),
        P(ALL, None),
        P(ALL, None),
        P(ALL, None, None),
        P(ALL, None, None),
        P(ALL, None, None),
    )
    return jax.shard_map(
        local,
        mesh=fine,
        in_specs=placed,
        out_specs=(P(ALL, None), P(ALL, None)),
        check_vma=False,
    )
```

```python
import math

import jax
import jax.numpy as jnp
from jax import lax
from jax.experimental import pallas as pl
from jax.experimental.pallas import tpu as pltpu
from jax.sharding import Mesh
from jax.sharding import PartitionSpec as P

D = 4096
QUERY_HEADS = 32
KEY_VALUE_HEADS = 2
HEAD_SIZE = 128
TOP = 2
BLOCK = 128
CAP = 8

LIST = ("y", "z")
EXPERT = ("x", "core")
CHIP = ("y", "z", "x")
ALL = ("y", "z", "x", "core")
SWAP = [(0, 1), (1, 0)]

masked_score = -1e30
MIB = 1 << 20


def attention_kernel(q_ref, prefix_ref, cand_ref, segment_col_ref, segment_row_ref, out_ref):
    block = pl.program_id(0)
    heads = q_ref.shape[1] // HEAD_SIZE
    factor = math.log2(math.e) / math.sqrt(HEAD_SIZE)
    start = pl.multiple_of(jnp.maximum(block - 1, 0) * BLOCK, BLOCK)
    window = cand_ref[pl.ds(start, 2 * BLOCK), :]
    query_at = block * BLOCK + lax.broadcasted_iota(jnp.int32, (BLOCK, 2 * BLOCK), 0)
    key_at = start + lax.broadcasted_iota(jnp.int32, (BLOCK, 2 * BLOCK), 1)
    key_segment = segment_row_ref[:, pl.ds(start, 2 * BLOCK)]
    allowed = (segment_col_ref[...] == key_segment) & (key_at <= query_at)
    prefix = prefix_ref[...]

    def with_ones(value):
        return jnp.concatenate([value, jnp.ones_like(value)], axis=1)

    prefix_key, prefix_value = prefix[:, :HEAD_SIZE], with_ones(prefix[:, HEAD_SIZE:])
    window_key, window_value = window[:, :HEAD_SIZE], with_ones(window[:, HEAD_SIZE:])
    contract = (((1,), (1,)), ((), ()))
    for head in range(heads):
        columns = slice(head * HEAD_SIZE, (head + 1) * HEAD_SIZE)
        q = q_ref[:, columns]
        far = lax.dot_general(q, prefix_key, contract, preferred_element_type=jnp.float32)
        near = lax.dot_general(q, window_key, contract, preferred_element_type=jnp.float32)
        near = jnp.where(allowed, near, masked_score)
        top = jnp.maximum(
            jnp.max(far, axis=-1, keepdims=True), jnp.max(near, axis=-1, keepdims=True)
        )
        far = jnp.exp2((far - top) * factor).astype(jnp.bfloat16)
        near = jnp.exp2((near - top) * factor).astype(jnp.bfloat16)
        total = jnp.dot(far, prefix_value, preferred_element_type=jnp.float32) + jnp.dot(
            near, window_value, preferred_element_type=jnp.float32
        )
        out_ref[:, columns] = (total[:, :HEAD_SIZE] / total[:, HEAD_SIZE:]).astype(jnp.bfloat16)


def attention(query, prefix, cand, segment):
    tokens, width = query.shape
    return pl.pallas_call(
        attention_kernel,
        out_shape=jax.ShapeDtypeStruct((tokens, width), jnp.bfloat16),
        grid=(tokens // BLOCK,),
        in_specs=[
            pl.BlockSpec((BLOCK, width), lambda i: (i, 0)),
            pl.BlockSpec(prefix.shape, lambda i: (0, 0)),
            pl.BlockSpec(cand.shape, lambda i: (0, 0)),
            pl.BlockSpec((BLOCK, 1), lambda i: (i, 0)),
            pl.BlockSpec((1, tokens), lambda i: (0, 0)),
        ],
        out_specs=pl.BlockSpec((BLOCK, width), lambda i: (i, 0)),
        compiler_params=pltpu.CompilerParams(vmem_limit_bytes=58 * MIB),
        name="attention",
    )(query, prefix, cand, segment.reshape(tokens, 1), segment.reshape(1, tokens))


def norm_pack_kernel(hidden_ref, attn_ref, gain_ref, row_ref, attended_ref, packed_ref):
    attended = (hidden_ref[...].astype(jnp.float32) + attn_ref[...].astype(jnp.float32)).astype(
        jnp.bfloat16
    )
    attended_ref[...] = attended
    widened = attended.astype(jnp.float32)
    mean_square = jnp.mean(widened * widened, axis=-1, keepdims=True)
    normed = (widened * lax.rsqrt(mean_square + 1e-06) * gain_ref[...].astype(jnp.float32)).astype(
        jnp.bfloat16
    )
    rows = packed_ref.shape[0]
    tokens = normed.shape[0]
    at = lax.broadcasted_iota(jnp.int32, (rows, tokens), 0)
    pick = (at == row_ref[0:1, :]) | (at == row_ref[1:2, :])
    pick = pick.astype(jnp.float32).astype(jnp.bfloat16)
    packed_ref[...] = jnp.dot(pick, normed, preferred_element_type=jnp.float32).astype(jnp.bfloat16)


def norm_pack(hidden, attn, gain, rows):
    tokens, width = hidden.shape
    slots = 64 * CAP
    return pl.pallas_call(
        norm_pack_kernel,
        out_shape=(
            jax.ShapeDtypeStruct((tokens, width), jnp.bfloat16),
            jax.ShapeDtypeStruct((slots, width), jnp.bfloat16),
        ),
        compiler_params=pltpu.CompilerParams(vmem_limit_bytes=58 * MIB),
        name="norm_pack",
    )(hidden, attn, gain.reshape(1, width), rows.T)


def combine_kernel(back_ref, row_ref, weight_ref, out_ref):
    tokens, slots = out_ref.shape[0], back_ref.shape[0]
    at = lax.broadcasted_iota(jnp.int32, (tokens, slots), 1)
    back = back_ref[...]
    total = None
    for k in range(TOP):
        pick = (at == row_ref[:, k : k + 1]).astype(jnp.float32).astype(jnp.bfloat16)
        term = weight_ref[:, k : k + 1] * jnp.dot(pick, back, preferred_element_type=jnp.float32)
        total = term if total is None else total + term
    out_ref[...] = total.astype(jnp.bfloat16)


def combine(back, rows, weights):
    slots, width = back.shape
    tokens = rows.shape[0]
    step = 1024
    return pl.pallas_call(
        combine_kernel,
        out_shape=jax.ShapeDtypeStruct((tokens, width), jnp.bfloat16),
        grid=(width // step,),
        in_specs=[
            pl.BlockSpec((slots, step), lambda i: (0, i)),
            pl.BlockSpec((tokens, TOP), lambda i: (0, 0)),
            pl.BlockSpec((tokens, TOP), lambda i: (0, 0)),
        ],
        out_specs=pl.BlockSpec((tokens, step), lambda i: (0, i)),
        compiler_params=pltpu.CompilerParams(vmem_limit_bytes=58 * MIB),
        name="combine",
    )(back, rows, weights)


def expert_kernel(
    x_hbm,
    gate_hbm,
    up_hbm,
    down_hbm,
    gate2_hbm,
    up2_hbm,
    down2_hbm,
    out_hbm,
    x_ref,
    gate_ref,
    up_ref,
    down_ref,
    act_ref,
    out_ref,
    x_sem,
    in_sem,
    down_sem,
    out_sem,
):
    hidden_units = gate_hbm.shape[1]
    width = x_hbm.shape[1]
    step, wide = 256, 1024
    per_half = hidden_units // step

    def first_copies(j):
        half, at = j // per_half, pl.ds((j % per_half) * step, step)
        to = pl.ds(j * step, step)
        gate, up = ((gate_hbm, up_hbm), (gate2_hbm, up2_hbm))[half]
        return (
            pltpu.make_async_copy(gate.at[:, at], gate_ref.at[:, to], in_sem.at[0, j]),
            pltpu.make_async_copy(up.at[:, at], up_ref.at[:, to], in_sem.at[1, j]),
        )

    def second_copies(j):
        at = pl.ds(j * wide, wide)
        return tuple(
            pltpu.make_async_copy(
                down.at[:, at],
                down_ref.at[pl.ds(half * hidden_units, hidden_units), at],
                down_sem.at[half, j],
            )
            for half, down in enumerate((down_hbm, down2_hbm))
        )

    def out_copy(j):
        at = pl.ds(j * wide, wide)
        return pltpu.make_async_copy(out_ref.at[:, at], out_hbm.at[:, at], out_sem.at[j])

    x_copy = pltpu.make_async_copy(x_hbm, x_ref, x_sem)
    loads = [first_copies(j) for j in range(2 * per_half)]
    loads += [second_copies(j) for j in range(width // wide)]
    ahead = 2
    x_copy.start()
    for copies in loads[:ahead]:
        for copy in copies:
            copy.start()
    x_copy.wait()
    for j, copies in enumerate(loads):
        for copy in loads[j + ahead] if j + ahead < len(loads) else ():
            copy.start()
        for copy in copies:
            copy.wait()
        if j < 2 * per_half:
            at = slice(j * step, (j + 1) * step)
            x = x_ref[...]
            gated = jnp.dot(x, gate_ref[:, at], preferred_element_type=jnp.float32)
            upward = jnp.dot(x, up_ref[:, at], preferred_element_type=jnp.float32)
            act_ref[:, at] = (gated / (1.0 + jnp.exp(-gated)) * upward).astype(jnp.bfloat16)
        else:
            j -= 2 * per_half
            at = slice(j * wide, (j + 1) * wide)
            out_ref[:, at] = jnp.dot(
                act_ref[...], down_ref[:, at], preferred_element_type=jnp.float32
            ).astype(jnp.bfloat16)
            out_copy(j).start()
    for j in range(width // wide):
        out_copy(j).wait()


def whole_expert(rows, own, swapped):
    slots, width = rows.shape
    both = 2 * own[0].shape[1]
    anywhere = pl.BlockSpec(memory_space=pl.ANY)
    return pl.pallas_call(
        expert_kernel,
        out_shape=jax.ShapeDtypeStruct(rows.shape, jnp.bfloat16),
        in_specs=[anywhere] * 7,
        out_specs=anywhere,
        scratch_shapes=[
            pltpu.VMEM((slots, width), jnp.bfloat16),
            pltpu.VMEM((width, both), jnp.bfloat16),
            pltpu.VMEM((width, both), jnp.bfloat16),
            pltpu.VMEM((both, width), jnp.bfloat16),
            pltpu.VMEM((slots, both), jnp.bfloat16),
            pltpu.VMEM((slots, width), jnp.bfloat16),
            pltpu.SemaphoreType.DMA,
            pltpu.SemaphoreType.DMA((2, 6)),
            pltpu.SemaphoreType.DMA((2, 4)),
            pltpu.SemaphoreType.DMA((4,)),
        ],
        compiler_params=pltpu.CompilerParams(vmem_limit_bytes=58 * MIB),
        name="whole_expert",
    )(rows, *own, *swapped)


def project_kernel(heads_ref, weight_ref, out_ref):
    wide = weight_ref.shape[2]
    for piece in range(weight_ref.shape[0]):
        out_ref[:, piece * wide : (piece + 1) * wide] = jnp.dot(
            heads_ref[...], weight_ref[piece], preferred_element_type=jnp.float32
        ).astype(jnp.bfloat16)


def project(heads, weight):
    tokens, width = heads.shape
    pieces, _, wide = weight.shape
    step = 2
    return pl.pallas_call(
        project_kernel,
        out_shape=jax.ShapeDtypeStruct((tokens, pieces * wide), jnp.bfloat16),
        grid=(pieces // step,),
        in_specs=[
            pl.BlockSpec((tokens, width), lambda i: (0, 0)),
            pl.BlockSpec((step, width, wide), lambda i: (i, 0, 0)),
        ],
        out_specs=pl.BlockSpec((tokens, step * wide), lambda i: (0, i)),
        compiler_params=pltpu.CompilerParams(vmem_limit_bytes=58 * MIB),
        name="project",
    )(heads, weight)


def slots_of(routes):
    tok_dev = routes.shape[0]
    flat_routes = routes.reshape(-1)
    matched = (flat_routes[:, None] == jnp.arange(64, dtype=jnp.int32)[None, :]).astype(jnp.int32)
    slot_index = jnp.sum((jnp.cumsum(matched, axis=0) - matched) * matched, axis=1)
    return (flat_routes * CAP + slot_index).reshape(tok_dev, TOP)


def local(
    hidden,
    query,
    candidate_key_value,
    prefix_key_value,
    segment_ids,
    o_weight,
    norm_gain,
    routes,
    route_weights,
    w_gate,
    w_up,
    w_down,
):
    heads_dev = query.shape[1] // HEAD_SIZE
    expert_index = lax.axis_index("x") * 2 + lax.axis_index("core")
    head = (expert_index * heads_dev) // (QUERY_HEADS // KEY_VALUE_HEADS)

    def of_head(key_value):
        part = lax.dynamic_slice_in_dim(key_value, head * HEAD_SIZE, HEAD_SIZE, 2)
        return part.reshape(key_value.shape[0], 2 * HEAD_SIZE)

    own_prefix = of_head(prefix_key_value)
    n_list = lax.axis_size(LIST)
    prefix = lax.all_to_all(
        jnp.broadcast_to(own_prefix[None], (n_list,) + own_prefix.shape),
        LIST,
        split_axis=0,
        concat_axis=0,
        tiled=True,
    ).reshape(-1, 2 * HEAD_SIZE)
    wo_pieces = lax.all_gather(o_weight, LIST, axis=0, tiled=False)
    heads_out = attention(query, prefix, of_head(candidate_key_value), segment_ids[0])
    attn = lax.psum_scatter(
        project(heads_out, wo_pieces),
        EXPERT,
        scatter_dimension=0,
        tiled=True,
    )
    rows = slots_of(routes)
    attended, packed = norm_pack(hidden, attn, norm_gain, rows)

    def across(slots):
        return lax.all_to_all(
            slots.reshape(64, CAP, D), CHIP, split_axis=0, concat_axis=0, tiled=True
        ).reshape(64 * CAP, D)

    own = (w_gate[0], w_up[0], w_down[0])
    swapped = tuple(lax.ppermute(w, "core", SWAP) for w in own)
    back = across(whole_expert(across(packed), own, swapped))
    return attended, combine(back, rows, route_weights)


def solution(mesh):
    fine = Mesh(mesh.devices.reshape(4, 4, 4, 2), ALL)
    placed = (
        P(ALL, None),
        P(LIST, EXPERT),
        P(LIST, None, None),
        P(LIST, None, None),
        P(LIST, None),
        P(EXPERT, LIST),
        P(),
        P(ALL, None),
        P(ALL, None),
        P(ALL, None, None),
        P(ALL, None, None),
        P(ALL, None, None),
    )
    return jax.shard_map(
        local,
        mesh=fine,
        in_specs=placed,
        out_specs=(P(ALL, None), P(ALL, None)),
        check_vma=False,
    )
```

```python
import functools
import math

import jax
import jax.numpy as jnp
from jax import lax
from jax.experimental import pallas as pl
from jax.experimental.pallas import tpu as pltpu
from jax.sharding import Mesh
from jax.sharding import PartitionSpec as P

D = 4096
QUERY_HEADS = 32
KEY_VALUE_HEADS = 2
HEAD_SIZE = 128
TOP = 2
BLOCK = 128
CAP = 8

LIST = ("y", "z")
EXPERT = ("x", "core")
CHIP = ("y", "z", "x")
ALL = ("y", "z", "x", "core")
SWAP = [(0, 1), (1, 0)]

masked_score = -1e30
MIB = 1 << 20
EXPERT_MIB = 32


def attention_kernel(
    order_ref, q_ref, prefix_ref, cand_ref, segment_col_ref, segment_row_ref, out_ref
):
    block = order_ref[pl.program_id(0)]
    heads = q_ref.shape[1] // HEAD_SIZE
    factor = math.log2(math.e) / math.sqrt(HEAD_SIZE)
    start = pl.multiple_of(jnp.maximum(block - 1, 0) * BLOCK, BLOCK)
    window = cand_ref[pl.ds(start, 2 * BLOCK), :]
    query_at = block * BLOCK + lax.broadcasted_iota(jnp.int32, (BLOCK, 2 * BLOCK), 0)
    key_at = start + lax.broadcasted_iota(jnp.int32, (BLOCK, 2 * BLOCK), 1)
    key_segment = segment_row_ref[:, pl.ds(start, 2 * BLOCK)]
    allowed = (segment_col_ref[...] == key_segment) & (key_at <= query_at)
    prefix = prefix_ref[...]

    def with_ones(value):
        return jnp.concatenate([value, jnp.ones_like(value)], axis=1)

    prefix_key, prefix_value = prefix[:, :HEAD_SIZE], with_ones(prefix[:, HEAD_SIZE:])
    window_key, window_value = window[:, :HEAD_SIZE], with_ones(window[:, HEAD_SIZE:])
    contract = (((1,), (1,)), ((), ()))
    for head in range(heads):
        columns = slice(head * HEAD_SIZE, (head + 1) * HEAD_SIZE)
        q = q_ref[:, columns]
        far = lax.dot_general(q, prefix_key, contract, preferred_element_type=jnp.float32)
        near = lax.dot_general(q, window_key, contract, preferred_element_type=jnp.float32)
        near = jnp.where(allowed, near, masked_score)
        top = jnp.maximum(
            jnp.max(far, axis=-1, keepdims=True), jnp.max(near, axis=-1, keepdims=True)
        )
        far = jnp.exp2((far - top) * factor).astype(jnp.bfloat16)
        near = jnp.exp2((near - top) * factor).astype(jnp.bfloat16)
        total = jnp.dot(far, prefix_value, preferred_element_type=jnp.float32) + jnp.dot(
            near, window_value, preferred_element_type=jnp.float32
        )
        out_ref[:, columns] = (total[:, :HEAD_SIZE] / total[:, HEAD_SIZE:]).astype(jnp.bfloat16)


def attention(query, prefix, cand, segment, order):
    tokens, width = query.shape
    return pl.pallas_call(
        attention_kernel,
        out_shape=jax.ShapeDtypeStruct((tokens, width), jnp.bfloat16),
        grid_spec=pltpu.PrefetchScalarGridSpec(
            num_scalar_prefetch=1,
            grid=(tokens // BLOCK,),
            in_specs=[
                pl.BlockSpec((BLOCK, width), lambda i, order: (order[i], 0)),
                pl.BlockSpec(prefix.shape, lambda i, order: (0, 0)),
                pl.BlockSpec(cand.shape, lambda i, order: (0, 0)),
                pl.BlockSpec((BLOCK, 1), lambda i, order: (order[i], 0)),
                pl.BlockSpec((1, tokens), lambda i, order: (0, 0)),
            ],
            out_specs=pl.BlockSpec((BLOCK, width), lambda i, order: (i, 0)),
        ),
        compiler_params=pltpu.CompilerParams(vmem_limit_bytes=24 * MIB),
        name="attention",
    )(order, query, prefix, cand, segment.reshape(tokens, 1), segment.reshape(1, tokens))


def norm_pack_kernel(
    hidden_ref,
    keep_ref,
    swap_ref,
    left_up_ref,
    right_up_ref,
    left_down_ref,
    right_down_ref,
    gain_ref,
    row_ref,
    attended_ref,
    packed_ref,
):
    def wide(ref):
        return ref[...].astype(jnp.float32)

    ringed = jnp.concatenate(
        [wide(left_up_ref) + wide(left_down_ref), wide(right_up_ref) + wide(right_down_ref)],
        axis=1,
    )
    attended = (wide(hidden_ref) + (wide(keep_ref) + wide(swap_ref)) + ringed).astype(jnp.bfloat16)
    attended_ref[...] = attended
    widened = attended.astype(jnp.float32)
    mean_square = jnp.mean(widened * widened, axis=-1, keepdims=True)
    normed = (widened * lax.rsqrt(mean_square + 1e-06) * gain_ref[...].astype(jnp.float32)).astype(
        jnp.bfloat16
    )
    rows = packed_ref.shape[0]
    tokens = normed.shape[0]
    at = lax.broadcasted_iota(jnp.int32, (rows, tokens), 0)
    pick = (at == row_ref[0:1, :]) | (at == row_ref[1:2, :])
    pick = pick.astype(jnp.float32).astype(jnp.bfloat16)
    packed_ref[...] = jnp.dot(pick, normed, preferred_element_type=jnp.float32).astype(jnp.bfloat16)


def norm_pack(hidden, parts, gain, rows):
    tokens, width = hidden.shape
    slots = 64 * CAP
    return pl.pallas_call(
        norm_pack_kernel,
        out_shape=(
            jax.ShapeDtypeStruct((tokens, width), jnp.bfloat16),
            jax.ShapeDtypeStruct((slots, width), jnp.bfloat16),
        ),
        compiler_params=pltpu.CompilerParams(vmem_limit_bytes=24 * MIB),
        name="norm_pack",
    )(hidden, *parts, gain.reshape(1, width), rows.T)


def combine_kernel(back_ref, row_ref, weight_ref, out_ref):
    tokens, slots = out_ref.shape[0], back_ref.shape[0]
    at = lax.broadcasted_iota(jnp.int32, (tokens, slots), 1)
    back = back_ref[...]
    total = None
    for k in range(TOP):
        pick = (at == row_ref[:, k : k + 1]).astype(jnp.float32).astype(jnp.bfloat16)
        term = weight_ref[:, k : k + 1] * jnp.dot(pick, back, preferred_element_type=jnp.float32)
        total = term if total is None else total + term
    out_ref[...] = total.astype(jnp.bfloat16)


def combine(back, rows, weights):
    slots, width = back.shape
    tokens = rows.shape[0]
    step = 1024
    return pl.pallas_call(
        combine_kernel,
        out_shape=jax.ShapeDtypeStruct((tokens, width), jnp.bfloat16),
        grid=(width // step,),
        in_specs=[
            pl.BlockSpec((slots, step), lambda i: (0, i)),
            pl.BlockSpec((tokens, TOP), lambda i: (0, 0)),
            pl.BlockSpec((tokens, TOP), lambda i: (0, 0)),
        ],
        out_specs=pl.BlockSpec((tokens, step), lambda i: (0, i)),
        compiler_params=pltpu.CompilerParams(vmem_limit_bytes=24 * MIB),
        name="combine",
    )(back, rows, weights)


def expert_kernel(
    x_ref,
    gate_ref,
    up_ref,
    down_hbm,
    gate2_hbm,
    up2_hbm,
    down2_hbm,
    out_ref,
    gate2_ref,
    up2_ref,
    down_ref,
    act_ref,
    in_sem,
    down_sem,
):
    hidden_units = gate_ref.shape[1]
    width = x_ref.shape[1]
    step, wide = 256, 1024
    per_half = hidden_units // step

    def first_copies(j):
        at = pl.ds(j * step, step)
        return (
            pltpu.make_async_copy(gate2_hbm.at[:, at], gate2_ref.at[:, at], in_sem.at[0, j]),
            pltpu.make_async_copy(up2_hbm.at[:, at], up2_ref.at[:, at], in_sem.at[1, j]),
        )

    def second_copies(j):
        at = pl.ds(j * wide, wide)
        return tuple(
            pltpu.make_async_copy(
                down.at[:, at],
                down_ref.at[pl.ds(half * hidden_units, hidden_units), at],
                down_sem.at[half, j],
            )
            for half, down in enumerate((down_hbm, down2_hbm))
        )

    loads = [()] * per_half + [first_copies(j) for j in range(per_half)]
    loads += [second_copies(j) for j in range(width // wide)]
    ahead = 3
    for j, copies in enumerate(loads):
        for copy in loads[j + ahead] if j + ahead < len(loads) else ():
            copy.start()
        for copy in copies:
            copy.wait()
        if j < 2 * per_half:
            gate, up = (gate_ref, up_ref) if j < per_half else (gate2_ref, up2_ref)
            at = slice((j % per_half) * step, (j % per_half + 1) * step)
            x = x_ref[...]
            gated = jnp.dot(x, gate[:, at], preferred_element_type=jnp.float32)
            upward = jnp.dot(x, up[:, at], preferred_element_type=jnp.float32)
            act_ref[:, j * step : (j + 1) * step] = (
                gated / (1.0 + jnp.exp(-gated)) * upward
            ).astype(jnp.bfloat16)
        else:
            at = slice((j - 2 * per_half) * wide, (j - 2 * per_half + 1) * wide)
            out_ref[:, at] = jnp.dot(
                act_ref[...], down_ref[:, at], preferred_element_type=jnp.float32
            ).astype(jnp.bfloat16)


def whole_expert(rows, own, swapped):
    slots, width = rows.shape
    units = own[0].shape[1]
    anywhere = pl.BlockSpec(memory_space=pl.ANY)
    whole = pl.BlockSpec(memory_space=pltpu.VMEM)
    return pl.pallas_call(
        expert_kernel,
        out_shape=jax.ShapeDtypeStruct(rows.shape, jnp.bfloat16),
        in_specs=[whole] * 3 + [anywhere] * 4,
        out_specs=whole,
        scratch_shapes=[
            pltpu.VMEM((width, units), jnp.bfloat16),
            pltpu.VMEM((width, units), jnp.bfloat16),
            pltpu.VMEM((2 * units, width), jnp.bfloat16),
            pltpu.VMEM((slots, 2 * units), jnp.bfloat16),
            pltpu.SemaphoreType.DMA((2, 3)),
            pltpu.SemaphoreType.DMA((2, 4)),
        ],
        compiler_params=pltpu.CompilerParams(vmem_limit_bytes=EXPERT_MIB * MIB),
        name="whole_expert",
    )(rows, *own, *swapped)


def project_kernel(first, heads_ref, weight_ref, send_ref, keep_ref):
    wide = weight_ref.shape[2]
    half = send_ref.shape[0]
    heads = heads_ref[first : first + 2 * half, :]
    for piece in range(weight_ref.shape[0]):
        at = slice(piece * wide, (piece + 1) * wide)
        out = jnp.dot(heads, weight_ref[piece], preferred_element_type=jnp.float32).astype(
            jnp.bfloat16
        )
        send_ref[:, at] = out[:half]
        keep_ref[:, at] = out[half:]


def project(heads, weight, tokens, first):
    width = heads.shape[1]
    pieces, _, wide = weight.shape
    half = jax.ShapeDtypeStruct((tokens // 2, pieces * wide), jnp.bfloat16)
    whole = pl.BlockSpec(memory_space=pltpu.VMEM)
    return pl.pallas_call(
        functools.partial(project_kernel, first),
        out_shape=(half, half),
        in_specs=[whole, whole],
        out_specs=(whole, whole),
        compiler_params=pltpu.CompilerParams(vmem_limit_bytes=24 * MIB),
        cost_estimate=pl.CostEstimate(
            flops=2 * tokens * width * pieces * wide,
            bytes_accessed=2 * (width + tokens) * pieces * wide,
            transcendentals=0,
        ),
        name="project",
    )(heads, weight)


def added(*terms):
    total = terms[0].astype(jnp.float32)
    for term in terms[1:]:
        total = total + term.astype(jnp.float32)
    return total.astype(jnp.bfloat16)


def reduce_over_experts(heads_out, wo_pieces):
    mid = D // 2

    def swapped(part):
        return lax.ppermute(part, "core", SWAP)

    def up(part):
        return lax.ppermute(part, "x", [(i, (i + 1) % 4) for i in range(4)])

    def down(part):
        return lax.ppermute(part, "x", [(i, (i - 1) % 4) for i in range(4)])

    far_send, far_keep = project(heads_out, wo_pieces, 2 * BLOCK, 4 * BLOCK)
    far_send, heads_out = lax.optimization_barrier((far_send, heads_out))
    far_swap = swapped(far_send)
    next_send, next_keep = project(heads_out, wo_pieces, 4 * BLOCK, 0)
    next_send, heads_out = lax.optimization_barrier((next_send, heads_out))
    next_swap = swapped(next_send)
    far_up = up(added(far_keep[:, :mid], far_swap[:, :mid]))
    far_down = down(added(far_keep[:, mid:], far_swap[:, mid:]))
    right_up = up(added(next_keep[:BLOCK, mid:], next_swap[:BLOCK, mid:]))
    left_down = down(added(next_keep[BLOCK:, :mid], next_swap[BLOCK:, :mid]))
    own_send, own_keep = project(heads_out, wo_pieces, 2 * BLOCK, 6 * BLOCK)
    own_swap = swapped(own_send)
    far_up, far_down, next_keep, next_swap = lax.optimization_barrier(
        (far_up, far_down, next_keep, next_swap)
    )
    left_up = up(added(next_keep[:BLOCK, :mid], next_swap[:BLOCK, :mid], far_up))
    right_down = down(added(next_keep[BLOCK:, mid:], next_swap[BLOCK:, mid:], far_down))
    return own_keep, own_swap, left_up, right_up, left_down, right_down


def slots_of(routes):
    tok_dev = routes.shape[0]
    flat_routes = routes.reshape(-1)
    matched = (flat_routes[:, None] == jnp.arange(64, dtype=jnp.int32)[None, :]).astype(jnp.int32)
    slot_index = jnp.sum((jnp.cumsum(matched, axis=0) - matched) * matched, axis=1)
    return (flat_routes * CAP + slot_index).reshape(tok_dev, TOP)


def local(
    hidden,
    query,
    candidate_key_value,
    prefix_key_value,
    segment_ids,
    o_weight,
    norm_gain,
    routes,
    route_weights,
    w_gate,
    w_up,
    w_down,
):
    heads_dev = query.shape[1] // HEAD_SIZE
    expert_index = lax.axis_index("x") * 2 + lax.axis_index("core")
    head = (expert_index * heads_dev) // (QUERY_HEADS // KEY_VALUE_HEADS)

    def of_head(key_value):
        part = lax.dynamic_slice_in_dim(key_value, head * HEAD_SIZE, HEAD_SIZE, 2)
        return part.reshape(key_value.shape[0], 2 * HEAD_SIZE)

    own_prefix = of_head(prefix_key_value)
    n_list = lax.axis_size(LIST)
    prefix = lax.all_to_all(
        jnp.broadcast_to(own_prefix[None], (n_list,) + own_prefix.shape),
        LIST,
        split_axis=0,
        concat_axis=0,
        tiled=True,
    ).reshape(-1, 2 * HEAD_SIZE)
    wo_pieces = lax.all_gather(o_weight, LIST, axis=0, tiled=False)
    at, core = lax.axis_index("x"), lax.axis_index("core")

    def block_of(step, own):
        return 2 * ((at + step) % 4) + (core if own else 1 - core)

    order = jnp.stack(
        [
            block_of(step, own)
            for step, own in (
                (1, False),
                (3, False),
                (1, True),
                (3, True),
                (2, False),
                (2, True),
                (0, False),
                (0, True),
            )
        ]
    ).astype(jnp.int32)
    heads_out = attention(query, prefix, of_head(candidate_key_value), segment_ids[0], order)
    own = (w_gate[0], w_up[0], w_down[0])
    swapped = tuple(lax.ppermute(w, "core", SWAP) for w in own)
    heads_out, swapped = lax.optimization_barrier((heads_out, swapped))
    parts = reduce_over_experts(heads_out, wo_pieces)
    rows = slots_of(routes)
    attended, packed = norm_pack(hidden, parts, norm_gain, rows)

    def across(slots):
        return lax.all_to_all(
            slots.reshape(64, CAP, D), CHIP, split_axis=0, concat_axis=0, tiled=True
        ).reshape(64 * CAP, D)

    back = across(whole_expert(across(packed), own, swapped))
    return attended, combine(back, rows, route_weights)


def solution(mesh):
    fine = Mesh(mesh.devices.reshape(4, 4, 4, 2), ALL)
    placed = (
        P(ALL, None),
        P(LIST, EXPERT),
        P(LIST, None, None),
        P(LIST, None, None),
        P(LIST, None),
        P(EXPERT, LIST),
        P(),
        P(ALL, None),
        P(ALL, None),
        P(ALL, None, None),
        P(ALL, None, None),
        P(ALL, None, None),
    )
    return jax.shard_map(
        local,
        mesh=fine,
        in_specs=placed,
        out_specs=(P(ALL, None), P(ALL, None)),
        check_vma=False,
    )
```

```python
import functools
import math

import jax
import jax.numpy as jnp
from jax import lax
from jax.experimental import pallas as pl
from jax.experimental.pallas import tpu as pltpu
from jax.sharding import Mesh
from jax.sharding import PartitionSpec as P

D = 4096
QUERY_HEADS = 32
KEY_VALUE_HEADS = 2
HEAD_SIZE = 128
TOP = 2
BLOCK = 128
CAP = 8

LIST = ("y", "z")
EXPERT = ("x", "core")
CHIP = ("y", "z", "x")
ALL = ("y", "z", "x", "core")
SWAP = [(0, 1), (1, 0)]

masked_score = -1e30
MIB = 1 << 20
EXPERT_MIB = 38
NEAR_FLOPS = 10**10


def attention_kernel(
    order_ref, q_ref, prefix_ref, cand_ref, segment_col_ref, segment_row_ref, out_ref
):
    block = order_ref[pl.program_id(0)]
    heads = q_ref.shape[1] // HEAD_SIZE
    factor = math.log2(math.e) / math.sqrt(HEAD_SIZE)
    start = pl.multiple_of(jnp.maximum(block - 1, 0) * BLOCK, BLOCK)
    window = cand_ref[pl.ds(start, 2 * BLOCK), :]
    query_at = block * BLOCK + lax.broadcasted_iota(jnp.int32, (BLOCK, 2 * BLOCK), 0)
    key_at = start + lax.broadcasted_iota(jnp.int32, (BLOCK, 2 * BLOCK), 1)
    key_segment = segment_row_ref[:, pl.ds(start, 2 * BLOCK)]
    allowed = (segment_col_ref[...] == key_segment) & (key_at <= query_at)
    prefix = prefix_ref[...]

    def with_ones(value):
        return jnp.concatenate([value, jnp.ones_like(value)], axis=1)

    prefix_key, prefix_value = prefix[:, :HEAD_SIZE], with_ones(prefix[:, HEAD_SIZE:])
    window_key, window_value = window[:, :HEAD_SIZE], with_ones(window[:, HEAD_SIZE:])
    contract = (((1,), (1,)), ((), ()))
    for head in range(heads):
        columns = slice(head * HEAD_SIZE, (head + 1) * HEAD_SIZE)
        q = q_ref[:, columns]
        far = lax.dot_general(q, prefix_key, contract, preferred_element_type=jnp.float32)
        near = lax.dot_general(q, window_key, contract, preferred_element_type=jnp.float32)
        near = jnp.where(allowed, near, masked_score)
        top = jnp.maximum(
            jnp.max(far, axis=-1, keepdims=True), jnp.max(near, axis=-1, keepdims=True)
        )
        far = jnp.exp2((far - top) * factor).astype(jnp.bfloat16)
        near = jnp.exp2((near - top) * factor).astype(jnp.bfloat16)
        total = jnp.dot(far, prefix_value, preferred_element_type=jnp.float32) + jnp.dot(
            near, window_value, preferred_element_type=jnp.float32
        )
        out_ref[:, columns] = (total[:, :HEAD_SIZE] / total[:, HEAD_SIZE:]).astype(jnp.bfloat16)


def attention(query, prefix, cand, segment, order):
    tokens, width = query.shape
    return pl.pallas_call(
        attention_kernel,
        out_shape=jax.ShapeDtypeStruct((tokens, width), jnp.bfloat16),
        grid_spec=pltpu.PrefetchScalarGridSpec(
            num_scalar_prefetch=1,
            grid=(tokens // BLOCK,),
            in_specs=[
                pl.BlockSpec((BLOCK, width), lambda i, order: (order[i], 0)),
                pl.BlockSpec(prefix.shape, lambda i, order: (0, 0)),
                pl.BlockSpec(cand.shape, lambda i, order: (0, 0)),
                pl.BlockSpec((BLOCK, 1), lambda i, order: (order[i], 0)),
                pl.BlockSpec((1, tokens), lambda i, order: (0, 0)),
            ],
            out_specs=pl.BlockSpec((BLOCK, width), lambda i, order: (i, 0)),
        ),
        compiler_params=pltpu.CompilerParams(vmem_limit_bytes=24 * MIB),
        name="attention",
    )(order, query, prefix, cand, segment.reshape(tokens, 1), segment.reshape(1, tokens))


def near_sum_kernel(hidden_ref, keep_ref, swap_ref, left_down_ref, right_up_ref, out_ref):
    mid = left_down_ref.shape[1]
    for at, near in ((slice(0, mid), left_down_ref), (slice(mid, 2 * mid), right_up_ref)):
        own = keep_ref[:, at].astype(jnp.float32) + swap_ref[:, at].astype(jnp.float32)
        out_ref[:, at] = (hidden_ref[:, at].astype(jnp.float32) + own) + near[...].astype(
            jnp.float32
        )


def near_sum(hidden, keep, swap, left_down, right_up):
    whole = pl.BlockSpec(memory_space=pltpu.VMEM)
    return pl.pallas_call(
        near_sum_kernel,
        out_shape=jax.ShapeDtypeStruct(hidden.shape, jnp.float32),
        in_specs=[whole] * 5,
        out_specs=whole,
        compiler_params=pltpu.CompilerParams(vmem_limit_bytes=24 * MIB),
        cost_estimate=pl.CostEstimate(
            flops=NEAR_FLOPS, bytes_accessed=8 * MIB, transcendentals=0
        ),
        name="near_sum",
    )(hidden, keep, swap, left_down, right_up)


def norm_pack_kernel(
    near_ref,
    left_up_ref,
    right_down_ref,
    gain_ref,
    row_ref,
    weight_ref,
    attended_ref,
    packed_ref,
    weight_out_ref,
):
    weight_out_ref[...] = weight_ref[...]
    ringed = jnp.concatenate(
        [left_up_ref[...].astype(jnp.float32), right_down_ref[...].astype(jnp.float32)], axis=1
    )
    attended = (near_ref[...] + ringed).astype(jnp.bfloat16)
    attended_ref[...] = attended
    widened = attended.astype(jnp.float32)
    mean_square = jnp.mean(widened * widened, axis=-1, keepdims=True)
    normed = (widened * lax.rsqrt(mean_square + 1e-06) * gain_ref[...].astype(jnp.float32)).astype(
        jnp.bfloat16
    )
    rows = packed_ref.shape[0]
    tokens = normed.shape[0]
    at = lax.broadcasted_iota(jnp.int32, (rows, tokens), 0)
    pick = (at == row_ref[0:1, :]) | (at == row_ref[1:2, :])
    pick = pick.astype(jnp.float32).astype(jnp.bfloat16)
    packed_ref[...] = jnp.dot(pick, normed, preferred_element_type=jnp.float32).astype(jnp.bfloat16)


def norm_pack(near, left_up, right_down, gain, rows, weights):
    tokens, width = near.shape
    slots = 64 * CAP
    whole = pl.BlockSpec(memory_space=pltpu.VMEM)
    return pl.pallas_call(
        norm_pack_kernel,
        out_shape=(
            jax.ShapeDtypeStruct((tokens, width), jnp.bfloat16),
            jax.ShapeDtypeStruct((slots, width), jnp.bfloat16),
            jax.ShapeDtypeStruct(weights.shape, jnp.float32),
        ),
        in_specs=[whole] * 6,
        out_specs=(whole, whole, whole),
        compiler_params=pltpu.CompilerParams(vmem_limit_bytes=24 * MIB),
        name="norm_pack",
    )(near, left_up, right_down, gain.reshape(1, width), rows.T, weights)


def combine_kernel(back_ref, row_ref, weight_ref, out_ref):
    tokens, slots = out_ref.shape[0], back_ref.shape[0]
    at = lax.broadcasted_iota(jnp.int32, (tokens, slots), 1)
    back = back_ref[...]
    total = None
    for k in range(TOP):
        pick = (at == row_ref[:, k : k + 1]).astype(jnp.float32).astype(jnp.bfloat16)
        term = weight_ref[:, k : k + 1] * jnp.dot(pick, back, preferred_element_type=jnp.float32)
        total = term if total is None else total + term
    out_ref[...] = total.astype(jnp.bfloat16)


def combine(back, rows, weights):
    whole = pl.BlockSpec(memory_space=pltpu.VMEM)
    return pl.pallas_call(
        combine_kernel,
        out_shape=jax.ShapeDtypeStruct((rows.shape[0], back.shape[1]), jnp.bfloat16),
        in_specs=[whole] * 3,
        out_specs=whole,
        compiler_params=pltpu.CompilerParams(vmem_limit_bytes=24 * MIB),
        name="combine",
    )(back, rows, weights)


def expert_kernel(
    x_ref,
    gate_ref,
    up_hbm,
    down_hbm,
    gate2_hbm,
    up2_hbm,
    down2_hbm,
    out_ref,
    up_ref,
    gate2_ref,
    up2_ref,
    down_ref,
    act_ref,
    in_sem,
    down_sem,
):
    hidden_units = gate_ref.shape[1]
    width = x_ref.shape[1]
    step, wide = 256, 1024
    per_half = hidden_units // step

    def own_copies(j):
        at = pl.ds(j * step, step)
        return (pltpu.make_async_copy(up_hbm.at[:, at], up_ref.at[:, at], in_sem.at[2, j]),)

    def first_copies(j):
        at = pl.ds(j * step, step)
        return (
            pltpu.make_async_copy(gate2_hbm.at[:, at], gate2_ref.at[:, at], in_sem.at[0, j]),
            pltpu.make_async_copy(up2_hbm.at[:, at], up2_ref.at[:, at], in_sem.at[1, j]),
        )

    def second_copies(j):
        at = pl.ds(j * wide, wide)
        return tuple(
            pltpu.make_async_copy(
                down.at[:, at],
                down_ref.at[pl.ds(half * hidden_units, hidden_units), at],
                down_sem.at[half, j],
            )
            for half, down in enumerate((down_hbm, down2_hbm))
        )

    loads = [own_copies(j) for j in range(per_half)]
    loads += [first_copies(j) for j in range(per_half)]
    loads += [second_copies(j) for j in range(width // wide)]
    ahead = 2
    for copies in loads[:ahead]:
        for copy in copies:
            copy.start()
    for j, copies in enumerate(loads):
        for copy in loads[j + ahead] if j + ahead < len(loads) else ():
            copy.start()
        if j >= per_half:
            for copy in copies:
                copy.wait()
        if j < 2 * per_half:
            gate, up = (gate_ref, up_ref) if j < per_half else (gate2_ref, up2_ref)
            at = slice((j % per_half) * step, (j % per_half + 1) * step)
            x = x_ref[...]
            gated = jnp.dot(x, gate[:, at], preferred_element_type=jnp.float32)
            if j < per_half:
                for copy in copies:
                    copy.wait()
            upward = jnp.dot(x, up[:, at], preferred_element_type=jnp.float32)
            act_ref[:, j * step : (j + 1) * step] = (
                gated / (1.0 + jnp.exp(-gated)) * upward
            ).astype(jnp.bfloat16)
        else:
            at = slice((j - 2 * per_half) * wide, (j - 2 * per_half + 1) * wide)
            out_ref[:, at] = jnp.dot(
                act_ref[...], down_ref[:, at], preferred_element_type=jnp.float32
            ).astype(jnp.bfloat16)


def whole_expert(rows, own, swapped):
    slots, width = rows.shape
    units = own[0].shape[1]
    anywhere = pl.BlockSpec(memory_space=pl.ANY)
    whole = pl.BlockSpec(memory_space=pltpu.VMEM)
    return pl.pallas_call(
        expert_kernel,
        out_shape=jax.ShapeDtypeStruct(rows.shape, jnp.bfloat16),
        in_specs=[whole] * 2 + [anywhere] * 5,
        out_specs=whole,
        scratch_shapes=[
            pltpu.VMEM((width, units), jnp.bfloat16),
            pltpu.VMEM((width, units), jnp.bfloat16),
            pltpu.VMEM((width, units), jnp.bfloat16),
            pltpu.VMEM((2 * units, width), jnp.bfloat16),
            pltpu.VMEM((slots, 2 * units), jnp.bfloat16),
            pltpu.SemaphoreType.DMA((3, 3)),
            pltpu.SemaphoreType.DMA((2, 4)),
        ],
        compiler_params=pltpu.CompilerParams(vmem_limit_bytes=EXPERT_MIB * MIB),
        name="whole_expert",
    )(rows, *own, *swapped)


def project_kernel(first, heads_ref, weight_ref, send_ref, keep_ref):
    wide = weight_ref.shape[2]
    half = send_ref.shape[0]
    heads = heads_ref[first : first + 2 * half, :]
    for piece in range(weight_ref.shape[0]):
        at = slice(piece * wide, (piece + 1) * wide)
        out = jnp.dot(heads, weight_ref[piece], preferred_element_type=jnp.float32).astype(
            jnp.bfloat16
        )
        send_ref[:, at] = out[:half]
        keep_ref[:, at] = out[half:]


def project(heads, weight, tokens, first):
    width = heads.shape[1]
    pieces, _, wide = weight.shape
    half = jax.ShapeDtypeStruct((tokens // 2, pieces * wide), jnp.bfloat16)
    whole = pl.BlockSpec(memory_space=pltpu.VMEM)
    return pl.pallas_call(
        functools.partial(project_kernel, first),
        out_shape=(half, half),
        in_specs=[whole, whole],
        out_specs=(whole, whole),
        compiler_params=pltpu.CompilerParams(vmem_limit_bytes=24 * MIB),
        cost_estimate=pl.CostEstimate(
            flops=1, bytes_accessed=2 * (width + tokens) * pieces * wide, transcendentals=0
        ),
        name="project",
    )(heads, weight)


def added(*terms):
    total = terms[0].astype(jnp.float32)
    for term in terms[1:]:
        total = total + term.astype(jnp.float32)
    return total.astype(jnp.bfloat16)


def reduce_over_experts(heads_out, wo_pieces):
    mid = D // 2

    def swapped(part):
        return lax.ppermute(part, "core", SWAP)

    def up(part):
        return lax.ppermute(part, "x", [(i, (i + 1) % 4) for i in range(4)])

    def down(part):
        return lax.ppermute(part, "x", [(i, (i - 1) % 4) for i in range(4)])

    far_send, far_keep = project(heads_out, wo_pieces, 2 * BLOCK, 4 * BLOCK)
    far_send, heads_out = lax.optimization_barrier((far_send, heads_out))
    far_swap = swapped(far_send)
    next_send, next_keep = project(heads_out, wo_pieces, 4 * BLOCK, 0)
    next_send, heads_out = lax.optimization_barrier((next_send, heads_out))
    next_swap = swapped(next_send)
    far_up = up(added(far_keep[:, :mid], far_swap[:, :mid]))
    far_down = down(added(far_keep[:, mid:], far_swap[:, mid:]))
    right_up = up(added(next_keep[:BLOCK, mid:], next_swap[:BLOCK, mid:]))
    left_down = down(added(next_keep[BLOCK:, :mid], next_swap[BLOCK:, :mid]))
    own_send, own_keep = project(heads_out, wo_pieces, 2 * BLOCK, 6 * BLOCK)
    own_swap = swapped(own_send)
    far_up, far_down, next_keep, next_swap = lax.optimization_barrier(
        (far_up, far_down, next_keep, next_swap)
    )
    left_up = up(added(next_keep[:BLOCK, :mid], next_swap[:BLOCK, :mid], far_up))
    right_down = down(added(next_keep[BLOCK:, mid:], next_swap[BLOCK:, mid:], far_down))
    return own_keep, own_swap, left_up, right_up, left_down, right_down


def slots_of(routes):
    tok_dev = routes.shape[0]
    flat_routes = routes.reshape(-1)
    matched = (flat_routes[:, None] == jnp.arange(64, dtype=jnp.int32)[None, :]).astype(jnp.int32)
    slot_index = jnp.sum((jnp.cumsum(matched, axis=0) - matched) * matched, axis=1)
    return (flat_routes * CAP + slot_index).reshape(tok_dev, TOP)


def local(
    hidden,
    query,
    candidate_key_value,
    prefix_key_value,
    segment_ids,
    o_weight,
    norm_gain,
    routes,
    route_weights,
    w_gate,
    w_up,
    w_down,
):
    heads_dev = query.shape[1] // HEAD_SIZE
    expert_index = lax.axis_index("x") * 2 + lax.axis_index("core")
    head = (expert_index * heads_dev) // (QUERY_HEADS // KEY_VALUE_HEADS)

    def of_head(key_value):
        part = lax.dynamic_slice_in_dim(key_value, head * HEAD_SIZE, HEAD_SIZE, 2)
        return part.reshape(key_value.shape[0], 2 * HEAD_SIZE)

    own_prefix = of_head(prefix_key_value)
    n_list = lax.axis_size(LIST)
    prefix = lax.all_to_all(
        jnp.broadcast_to(own_prefix[None], (n_list,) + own_prefix.shape),
        LIST,
        split_axis=0,
        concat_axis=0,
        tiled=True,
    ).reshape(-1, 2 * HEAD_SIZE)
    wo_pieces = lax.all_gather(o_weight, LIST, axis=0, tiled=False)
    at, core = lax.axis_index("x"), lax.axis_index("core")

    def block_of(step, own):
        return 2 * ((at + step) % 4) + (core if own else 1 - core)

    order = jnp.stack(
        [
            block_of(step, own)
            for step, own in (
                (1, False),
                (3, False),
                (1, True),
                (3, True),
                (2, False),
                (2, True),
                (0, False),
                (0, True),
            )
        ]
    ).astype(jnp.int32)
    heads_out = attention(query, prefix, of_head(candidate_key_value), segment_ids[0], order)
    own = (w_gate[0], w_up[0], w_down[0])
    swapped = tuple(lax.ppermute(w, "core", SWAP) for w in own)
    heads_out, swapped = lax.optimization_barrier((heads_out, swapped))
    parts = reduce_over_experts(heads_out, wo_pieces)
    rows = slots_of(routes)
    own_keep, own_swap, left_up, right_up, left_down, right_down = parts
    near = near_sum(hidden, own_keep, own_swap, left_down, right_up)
    attended, packed, weights = norm_pack(
        near, left_up, right_down, norm_gain, rows, route_weights
    )

    def across(slots):
        return lax.all_to_all(
            slots.reshape(64, CAP, D), CHIP, split_axis=0, concat_axis=0, tiled=True
        ).reshape(64 * CAP, D)

    back = across(whole_expert(across(packed), own, swapped))
    return attended, combine(back, rows, weights)


def solution(mesh):
    fine = Mesh(mesh.devices.reshape(4, 4, 4, 2), ALL)
    placed = (
        P(ALL, None),
        P(LIST, EXPERT),
        P(LIST, None, None),
        P(LIST, None, None),
        P(LIST, None),
        P(EXPERT, LIST),
        P(),
        P(ALL, None),
        P(ALL, None),
        P(ALL, None, None),
        P(ALL, None, None),
        P(ALL, None, None),
    )
    return jax.shard_map(
        local,
        mesh=fine,
        in_specs=placed,
        out_specs=(P(ALL, None), P(ALL, None)),
        check_vma=False,
    )
```

```python
import functools
import math

import jax
import jax.numpy as jnp
from jax import lax
from jax.experimental import pallas as pl
from jax.experimental.pallas import tpu as pltpu
from jax.sharding import Mesh
from jax.sharding import PartitionSpec as P

D = 4096
QUERY_HEADS = 32
KEY_VALUE_HEADS = 2
HEAD_SIZE = 128
TOP = 2
BLOCK = 128
CAP = 8

LIST = ("y", "z")
EXPERT = ("x", "core")
CHIP = ("y", "z", "x")
ALL = ("y", "z", "x", "core")
SWAP = [(0, 1), (1, 0)]

masked_score = -1e30
MIB = 1 << 20
EXPERT_MIB = 38
NEAR_FLOPS = 10**10


def attention_kernel(
    order_ref, q_ref, prefix_ref, cand_ref, segment_col_ref, segment_row_ref, out_ref
):
    block = order_ref[pl.program_id(0)]
    heads = q_ref.shape[1] // HEAD_SIZE
    factor = math.log2(math.e) / math.sqrt(HEAD_SIZE)
    start = pl.multiple_of(jnp.maximum(block - 1, 0) * BLOCK, BLOCK)
    window = cand_ref[pl.ds(start, 2 * BLOCK), :]
    query_at = block * BLOCK + lax.broadcasted_iota(jnp.int32, (BLOCK, 2 * BLOCK), 0)
    key_at = start + lax.broadcasted_iota(jnp.int32, (BLOCK, 2 * BLOCK), 1)
    key_segment = segment_row_ref[:, pl.ds(start, 2 * BLOCK)]
    allowed = (segment_col_ref[...] == key_segment) & (key_at <= query_at)
    prefix = prefix_ref[...]

    def with_ones(value):
        return jnp.concatenate([value, jnp.ones_like(value)], axis=1)

    prefix_key, prefix_value = prefix[:, :HEAD_SIZE], with_ones(prefix[:, HEAD_SIZE:])
    window_key, window_value = window[:, :HEAD_SIZE], with_ones(window[:, HEAD_SIZE:])
    contract = (((1,), (1,)), ((), ()))
    for head in range(heads):
        columns = slice(head * HEAD_SIZE, (head + 1) * HEAD_SIZE)
        q = q_ref[:, columns]
        far = lax.dot_general(q, prefix_key, contract, preferred_element_type=jnp.float32)
        near = lax.dot_general(q, window_key, contract, preferred_element_type=jnp.float32)
        near = jnp.where(allowed, near, masked_score)
        top = jnp.maximum(
            jnp.max(far, axis=-1, keepdims=True), jnp.max(near, axis=-1, keepdims=True)
        )
        far = jnp.exp2((far - top) * factor).astype(jnp.bfloat16)
        near = jnp.exp2((near - top) * factor).astype(jnp.bfloat16)
        total = jnp.dot(far, prefix_value, preferred_element_type=jnp.float32) + jnp.dot(
            near, window_value, preferred_element_type=jnp.float32
        )
        out_ref[:, columns] = (total[:, :HEAD_SIZE] / total[:, HEAD_SIZE:]).astype(jnp.bfloat16)


def attention(query, prefix, cand, segment, order):
    tokens, width = query.shape
    return pl.pallas_call(
        attention_kernel,
        out_shape=jax.ShapeDtypeStruct((tokens, width), jnp.bfloat16),
        grid_spec=pltpu.PrefetchScalarGridSpec(
            num_scalar_prefetch=1,
            grid=(tokens // BLOCK,),
            in_specs=[
                pl.BlockSpec((BLOCK, width), lambda i, order: (order[i], 0)),
                pl.BlockSpec(prefix.shape, lambda i, order: (0, 0)),
                pl.BlockSpec(cand.shape, lambda i, order: (0, 0)),
                pl.BlockSpec((BLOCK, 1), lambda i, order: (order[i], 0)),
                pl.BlockSpec((1, tokens), lambda i, order: (0, 0)),
            ],
            out_specs=pl.BlockSpec((BLOCK, width), lambda i, order: (i, 0)),
        ),
        compiler_params=pltpu.CompilerParams(vmem_limit_bytes=24 * MIB),
        name="attention",
    )(order, query, prefix, cand, segment.reshape(tokens, 1), segment.reshape(1, tokens))


def near_sum_kernel(hidden_ref, keep_ref, swap_ref, left_down_ref, right_up_ref, out_ref):
    mid = left_down_ref.shape[1]
    for at, near in ((slice(0, mid), left_down_ref), (slice(mid, 2 * mid), right_up_ref)):
        own = keep_ref[:, at].astype(jnp.float32) + swap_ref[:, at].astype(jnp.float32)
        out_ref[:, at] = (hidden_ref[:, at].astype(jnp.float32) + own) + near[...].astype(
            jnp.float32
        )


def near_sum(hidden, keep, swap, left_down, right_up):
    whole = pl.BlockSpec(memory_space=pltpu.VMEM)
    return pl.pallas_call(
        near_sum_kernel,
        out_shape=jax.ShapeDtypeStruct(hidden.shape, jnp.float32),
        in_specs=[whole] * 5,
        out_specs=whole,
        compiler_params=pltpu.CompilerParams(vmem_limit_bytes=24 * MIB),
        cost_estimate=pl.CostEstimate(
            flops=NEAR_FLOPS, bytes_accessed=8 * MIB, transcendentals=0
        ),
        name="near_sum",
    )(hidden, keep, swap, left_down, right_up)


def norm_pack_kernel(
    near_ref,
    left_up_ref,
    right_down_ref,
    gain_ref,
    row_ref,
    weight_ref,
    attended_ref,
    packed_ref,
    weight_out_ref,
):
    weight_out_ref[...] = weight_ref[...]
    ringed = jnp.concatenate(
        [left_up_ref[...].astype(jnp.float32), right_down_ref[...].astype(jnp.float32)], axis=1
    )
    attended = (near_ref[...] + ringed).astype(jnp.bfloat16)
    attended_ref[...] = attended
    widened = attended.astype(jnp.float32)
    mean_square = jnp.mean(widened * widened, axis=-1, keepdims=True)
    normed = (widened * lax.rsqrt(mean_square + 1e-06) * gain_ref[...].astype(jnp.float32)).astype(
        jnp.bfloat16
    )
    rows = packed_ref.shape[0]
    tokens = normed.shape[0]
    at = lax.broadcasted_iota(jnp.int32, (rows, tokens), 0)
    pick = (at == row_ref[0:1, :]) | (at == row_ref[1:2, :])
    pick = pick.astype(jnp.float32).astype(jnp.bfloat16)
    packed_ref[...] = jnp.dot(pick, normed, preferred_element_type=jnp.float32).astype(jnp.bfloat16)


def norm_pack(near, left_up, right_down, gain, rows_t, weights):
    tokens, width = near.shape
    slots = 64 * CAP
    whole = pl.BlockSpec(memory_space=pltpu.VMEM)
    return pl.pallas_call(
        norm_pack_kernel,
        out_shape=(
            jax.ShapeDtypeStruct((tokens, width), jnp.bfloat16),
            jax.ShapeDtypeStruct((slots, width), jnp.bfloat16),
            jax.ShapeDtypeStruct(weights.shape, jnp.float32),
        ),
        in_specs=[whole] * 6,
        out_specs=(whole, whole, whole),
        compiler_params=pltpu.CompilerParams(vmem_limit_bytes=24 * MIB),
        name="norm_pack",
    )(near, left_up, right_down, gain, rows_t, weights)


def combine_kernel(back_ref, row_ref, weight_ref, out_ref):
    tokens, slots = out_ref.shape[0], back_ref.shape[0]
    at = lax.broadcasted_iota(jnp.int32, (tokens, slots), 1)
    back = back_ref[...]
    total = None
    for k in range(TOP):
        pick = (at == row_ref[:, k : k + 1]).astype(jnp.float32).astype(jnp.bfloat16)
        term = weight_ref[:, k : k + 1] * jnp.dot(pick, back, preferred_element_type=jnp.float32)
        total = term if total is None else total + term
    out_ref[...] = total.astype(jnp.bfloat16)


def combine(back, rows, weights):
    whole = pl.BlockSpec(memory_space=pltpu.VMEM)
    return pl.pallas_call(
        combine_kernel,
        out_shape=jax.ShapeDtypeStruct((rows.shape[0], back.shape[1]), jnp.bfloat16),
        in_specs=[whole] * 3,
        out_specs=whole,
        compiler_params=pltpu.CompilerParams(vmem_limit_bytes=24 * MIB),
        name="combine",
    )(back, rows, weights)


def expert_kernel(
    x_ref,
    gate_ref,
    up_hbm,
    down_hbm,
    gate2_hbm,
    up2_hbm,
    down2_hbm,
    out_ref,
    up_ref,
    gate2_ref,
    up2_ref,
    down_ref,
    act_ref,
    in_sem,
    down_sem,
):
    hidden_units = gate_ref.shape[1]
    width = x_ref.shape[1]
    step, wide = 256, 1024
    per_half = hidden_units // step

    def own_copies(j):
        at = pl.ds(j * step, step)
        return (pltpu.make_async_copy(up_hbm.at[:, at], up_ref.at[:, at], in_sem.at[2, j]),)

    def first_copies(j):
        at = pl.ds(j * step, step)
        return (
            pltpu.make_async_copy(gate2_hbm.at[:, at], gate2_ref.at[:, at], in_sem.at[0, j]),
            pltpu.make_async_copy(up2_hbm.at[:, at], up2_ref.at[:, at], in_sem.at[1, j]),
        )

    def second_copies(j):
        at = pl.ds(j * wide, wide)
        return tuple(
            pltpu.make_async_copy(
                down.at[:, at],
                down_ref.at[pl.ds(half * hidden_units, hidden_units), at],
                down_sem.at[half, j],
            )
            for half, down in enumerate((down_hbm, down2_hbm))
        )

    loads = [own_copies(j) for j in range(per_half)]
    loads += [first_copies(j) for j in range(per_half)]
    loads += [second_copies(j) for j in range(width // wide)]
    ahead = 2
    for copies in loads[:ahead]:
        for copy in copies:
            copy.start()
    for j, copies in enumerate(loads):
        for copy in loads[j + ahead] if j + ahead < len(loads) else ():
            copy.start()
        if j >= per_half:
            for copy in copies:
                copy.wait()
        if j < 2 * per_half:
            gate, up = (gate_ref, up_ref) if j < per_half else (gate2_ref, up2_ref)
            at = slice((j % per_half) * step, (j % per_half + 1) * step)
            x = x_ref[...]
            gated = jnp.dot(x, gate[:, at], preferred_element_type=jnp.float32)
            if j < per_half:
                for copy in copies:
                    copy.wait()
            upward = jnp.dot(x, up[:, at], preferred_element_type=jnp.float32)
            act_ref[:, j * step : (j + 1) * step] = (
                gated / (1.0 + jnp.exp(-gated)) * upward
            ).astype(jnp.bfloat16)
        else:
            at = slice((j - 2 * per_half) * wide, (j - 2 * per_half + 1) * wide)
            out_ref[:, at] = jnp.dot(
                act_ref[...], down_ref[:, at], preferred_element_type=jnp.float32
            ).astype(jnp.bfloat16)


def whole_expert(rows, own, swapped):
    slots, width = rows.shape
    units = own[0].shape[1]
    anywhere = pl.BlockSpec(memory_space=pl.ANY)
    whole = pl.BlockSpec(memory_space=pltpu.VMEM)
    return pl.pallas_call(
        expert_kernel,
        out_shape=jax.ShapeDtypeStruct(rows.shape, jnp.bfloat16),
        in_specs=[whole] * 2 + [anywhere] * 5,
        out_specs=whole,
        scratch_shapes=[
            pltpu.VMEM((width, units), jnp.bfloat16),
            pltpu.VMEM((width, units), jnp.bfloat16),
            pltpu.VMEM((width, units), jnp.bfloat16),
            pltpu.VMEM((2 * units, width), jnp.bfloat16),
            pltpu.VMEM((slots, 2 * units), jnp.bfloat16),
            pltpu.SemaphoreType.DMA((3, 3)),
            pltpu.SemaphoreType.DMA((2, 4)),
        ],
        compiler_params=pltpu.CompilerParams(vmem_limit_bytes=EXPERT_MIB * MIB),
        name="whole_expert",
    )(rows, *own, *swapped)


def project_kernel(first, heads_ref, weight_ref, send_ref, keep_ref):
    wide = weight_ref.shape[2]
    half = send_ref.shape[0]
    heads = heads_ref[first : first + 2 * half, :]
    for piece in range(weight_ref.shape[0]):
        at = slice(piece * wide, (piece + 1) * wide)
        out = jnp.dot(heads, weight_ref[piece], preferred_element_type=jnp.float32).astype(
            jnp.bfloat16
        )
        send_ref[:, at] = out[:half]
        keep_ref[:, at] = out[half:]


def project(heads, weight, tokens, first):
    width = heads.shape[1]
    pieces, _, wide = weight.shape
    half = jax.ShapeDtypeStruct((tokens // 2, pieces * wide), jnp.bfloat16)
    whole = pl.BlockSpec(memory_space=pltpu.VMEM)
    return pl.pallas_call(
        functools.partial(project_kernel, first),
        out_shape=(half, half),
        in_specs=[whole, whole],
        out_specs=(whole, whole),
        compiler_params=pltpu.CompilerParams(vmem_limit_bytes=24 * MIB),
        cost_estimate=pl.CostEstimate(
            flops=1, bytes_accessed=2 * (width + tokens) * pieces * wide, transcendentals=0
        ),
        name="project",
    )(heads, weight)


def added(*terms):
    total = terms[0].astype(jnp.float32)
    for term in terms[1:]:
        total = total + term.astype(jnp.float32)
    return total.astype(jnp.bfloat16)


def reduce_over_experts(heads_out, wo_pieces):
    mid = D // 2

    def swapped(part):
        return lax.ppermute(part, "core", SWAP)

    def up(part):
        return lax.ppermute(part, "x", [(i, (i + 1) % 4) for i in range(4)])

    def down(part):
        return lax.ppermute(part, "x", [(i, (i - 1) % 4) for i in range(4)])

    far_send, far_keep = project(heads_out, wo_pieces, 2 * BLOCK, 4 * BLOCK)
    far_swap = swapped(far_send)
    far_left, far_right, heads_out = lax.optimization_barrier(
        (
            added(far_keep[:, :mid], far_swap[:, :mid]),
            added(far_keep[:, mid:], far_swap[:, mid:]),
            heads_out,
        )
    )
    far_up, far_down = up(far_left), down(far_right)
    next_send, next_keep = project(heads_out, wo_pieces, 4 * BLOCK, 0)
    next_send, heads_out = lax.optimization_barrier((next_send, heads_out))
    next_swap = swapped(next_send)
    right_up = up(added(next_keep[:BLOCK, mid:], next_swap[:BLOCK, mid:]))
    left_down = down(added(next_keep[BLOCK:, :mid], next_swap[BLOCK:, :mid]))
    own_send, own_keep = project(heads_out, wo_pieces, 2 * BLOCK, 6 * BLOCK)
    own_swap = swapped(own_send)
    far_up, far_down, next_keep, next_swap = lax.optimization_barrier(
        (far_up, far_down, next_keep, next_swap)
    )
    left_up = up(added(next_keep[:BLOCK, :mid], next_swap[:BLOCK, :mid], far_up))
    right_down = down(added(next_keep[BLOCK:, mid:], next_swap[BLOCK:, mid:], far_down))
    return own_keep, own_swap, left_up, right_up, left_down, right_down


def slots_of(routes):
    tok_dev = routes.shape[0]
    flat_routes = routes.reshape(-1)
    matched = (flat_routes[:, None] == jnp.arange(64, dtype=jnp.int32)[None, :]).astype(jnp.int32)
    slot_index = jnp.sum((jnp.cumsum(matched, axis=0) - matched) * matched, axis=1)
    return (flat_routes * CAP + slot_index).reshape(tok_dev, TOP)


def local(
    hidden,
    query,
    candidate_key_value,
    prefix_key_value,
    segment_ids,
    o_weight,
    norm_gain,
    routes,
    route_weights,
    w_gate,
    w_up,
    w_down,
):
    heads_dev = query.shape[1] // HEAD_SIZE
    expert_index = lax.axis_index("x") * 2 + lax.axis_index("core")
    head = (expert_index * heads_dev) // (QUERY_HEADS // KEY_VALUE_HEADS)

    def of_head(key_value):
        part = lax.dynamic_slice_in_dim(key_value, head * HEAD_SIZE, HEAD_SIZE, 2)
        return part.reshape(key_value.shape[0], 2 * HEAD_SIZE)

    own_prefix = of_head(prefix_key_value)
    n_list = lax.axis_size(LIST)
    prefix = lax.all_to_all(
        jnp.broadcast_to(own_prefix[None], (n_list,) + own_prefix.shape),
        LIST,
        split_axis=0,
        concat_axis=0,
        tiled=True,
    ).reshape(-1, 2 * HEAD_SIZE)
    wo_pieces = lax.all_gather(o_weight, LIST, axis=0, tiled=False)
    at, core = lax.axis_index("x"), lax.axis_index("core")

    def block_of(step, own):
        return 2 * ((at + step) % 4) + (core if own else 1 - core)

    order = jnp.stack(
        [
            block_of(step, own)
            for step, own in (
                (1, False),
                (3, False),
                (1, True),
                (3, True),
                (2, False),
                (2, True),
                (0, False),
                (0, True),
            )
        ]
    ).astype(jnp.int32)
    heads_out = attention(query, prefix, of_head(candidate_key_value), segment_ids[0], order)
    own = (w_gate[0], w_up[0], w_down[0])
    swapped = tuple(lax.ppermute(w, "core", SWAP) for w in own)
    rows = slots_of(routes)
    heads_out, swapped, rows, rows_t, gain = lax.optimization_barrier(
        (heads_out, swapped, rows, rows.T, norm_gain.reshape(1, D))
    )
    parts = reduce_over_experts(heads_out, wo_pieces)
    own_keep, own_swap, left_up, right_up, left_down, right_down = parts
    near = near_sum(hidden, own_keep, own_swap, left_down, right_up)
    attended, packed, weights = norm_pack(
        near, left_up, right_down, gain, rows_t, route_weights
    )

    def across(slots):
        return lax.all_to_all(
            slots.reshape(64, CAP, D), CHIP, split_axis=0, concat_axis=0, tiled=True
        ).reshape(64 * CAP, D)

    back = across(whole_expert(across(packed), own, swapped))
    return attended, combine(back, rows, weights)


def solution(mesh):
    fine = Mesh(mesh.devices.reshape(4, 4, 4, 2), ALL)
    placed = (
        P(ALL, None),
        P(LIST, EXPERT),
        P(LIST, None, None),
        P(LIST, None, None),
        P(LIST, None),
        P(EXPERT, LIST),
        P(),
        P(ALL, None),
        P(ALL, None),
        P(ALL, None, None),
        P(ALL, None, None),
        P(ALL, None, None),
    )
    return jax.shard_map(
        local,
        mesh=fine,
        in_specs=placed,
        out_specs=(P(ALL, None), P(ALL, None)),
        check_vma=False,
    )
```

```python
import functools
import math

import jax
import jax.numpy as jnp
from jax import lax
from jax.experimental import pallas as pl
from jax.experimental.pallas import tpu as pltpu
from jax.sharding import Mesh
from jax.sharding import PartitionSpec as P

D = 4096
QUERY_HEADS = 32
KEY_VALUE_HEADS = 2
HEAD_SIZE = 128
TOP = 2
BLOCK = 128
CAP = 8

LIST = ("y", "z")
EXPERT = ("x", "core")
CHIP = ("y", "z", "x")
ALL = ("y", "z", "x", "core")
SWAP = [(0, 1), (1, 0)]

masked_score = -1e30
MIB = 1 << 20
EXPERT_MIB = 38
NEAR_FLOPS = 10**10


def attention_kernel(
    order_ref, q_ref, prefix_ref, cand_ref, segment_col_ref, segment_row_ref, out_ref
):
    block = order_ref[pl.program_id(0)]
    heads = q_ref.shape[1] // HEAD_SIZE
    factor = math.log2(math.e) / math.sqrt(HEAD_SIZE)
    start = pl.multiple_of(jnp.maximum(block - 1, 0) * BLOCK, BLOCK)
    window = cand_ref[pl.ds(start, 2 * BLOCK), :]
    query_at = block * BLOCK + lax.broadcasted_iota(jnp.int32, (BLOCK, 2 * BLOCK), 0)
    key_at = start + lax.broadcasted_iota(jnp.int32, (BLOCK, 2 * BLOCK), 1)
    key_segment = segment_row_ref[:, pl.ds(start, 2 * BLOCK)]
    allowed = (segment_col_ref[...] == key_segment) & (key_at <= query_at)
    prefix = prefix_ref[...]

    def with_ones(value):
        return jnp.concatenate([value, jnp.ones_like(value)], axis=1)

    prefix_key, prefix_value = prefix[:, :HEAD_SIZE], with_ones(prefix[:, HEAD_SIZE:])
    window_key, window_value = window[:, :HEAD_SIZE], with_ones(window[:, HEAD_SIZE:])
    contract = (((1,), (1,)), ((), ()))
    for head in range(heads):
        columns = slice(head * HEAD_SIZE, (head + 1) * HEAD_SIZE)
        q = q_ref[:, columns]
        far = lax.dot_general(q, prefix_key, contract, preferred_element_type=jnp.float32)
        near = lax.dot_general(q, window_key, contract, preferred_element_type=jnp.float32)
        near = jnp.where(allowed, near, masked_score)
        top = jnp.maximum(
            jnp.max(far, axis=-1, keepdims=True), jnp.max(near, axis=-1, keepdims=True)
        )
        far = jnp.exp2((far - top) * factor).astype(jnp.bfloat16)
        near = jnp.exp2((near - top) * factor).astype(jnp.bfloat16)
        total = jnp.dot(far, prefix_value, preferred_element_type=jnp.float32) + jnp.dot(
            near, window_value, preferred_element_type=jnp.float32
        )
        out_ref[:, columns] = (total[:, :HEAD_SIZE] / total[:, HEAD_SIZE:]).astype(jnp.bfloat16)


def attention(query, prefix, cand, segment, order):
    tokens, width = query.shape
    return pl.pallas_call(
        attention_kernel,
        out_shape=jax.ShapeDtypeStruct((tokens, width), jnp.bfloat16),
        grid_spec=pltpu.PrefetchScalarGridSpec(
            num_scalar_prefetch=1,
            grid=(tokens // BLOCK,),
            in_specs=[
                pl.BlockSpec((BLOCK, width), lambda i, order: (order[i], 0)),
                pl.BlockSpec(prefix.shape, lambda i, order: (0, 0)),
                pl.BlockSpec(cand.shape, lambda i, order: (0, 0)),
                pl.BlockSpec((BLOCK, 1), lambda i, order: (order[i], 0)),
                pl.BlockSpec((1, tokens), lambda i, order: (0, 0)),
            ],
            out_specs=pl.BlockSpec((BLOCK, width), lambda i, order: (i, 0)),
        ),
        compiler_params=pltpu.CompilerParams(vmem_limit_bytes=24 * MIB),
        name="attention",
    )(order, query, prefix, cand, segment.reshape(tokens, 1), segment.reshape(1, tokens))


def near_sum_kernel(hidden_ref, keep_ref, swap_ref, left_down_ref, right_up_ref, out_ref):
    mid = left_down_ref.shape[1]
    for at, near in ((slice(0, mid), left_down_ref), (slice(mid, 2 * mid), right_up_ref)):
        own = keep_ref[:, at].astype(jnp.float32) + swap_ref[:, at].astype(jnp.float32)
        out_ref[:, at] = (hidden_ref[:, at].astype(jnp.float32) + own) + near[...].astype(
            jnp.float32
        )


def near_sum(hidden, keep, swap, left_down, right_up):
    whole = pl.BlockSpec(memory_space=pltpu.VMEM)
    return pl.pallas_call(
        near_sum_kernel,
        out_shape=jax.ShapeDtypeStruct(hidden.shape, jnp.float32),
        in_specs=[whole] * 5,
        out_specs=whole,
        compiler_params=pltpu.CompilerParams(vmem_limit_bytes=24 * MIB),
        cost_estimate=pl.CostEstimate(
            flops=NEAR_FLOPS, bytes_accessed=8 * MIB, transcendentals=0
        ),
        name="near_sum",
    )(hidden, keep, swap, left_down, right_up)


def norm_pack_kernel(
    near_ref,
    left_up_ref,
    right_down_ref,
    gain_ref,
    row_ref,
    weight_ref,
    attended_ref,
    packed_ref,
    weight_out_ref,
):
    weight_out_ref[...] = weight_ref[...]
    ringed = jnp.concatenate(
        [left_up_ref[...].astype(jnp.float32), right_down_ref[...].astype(jnp.float32)], axis=1
    )
    attended = (near_ref[...] + ringed).astype(jnp.bfloat16)
    attended_ref[...] = attended
    widened = attended.astype(jnp.float32)
    mean_square = jnp.mean(widened * widened, axis=-1, keepdims=True)
    normed = (widened * lax.rsqrt(mean_square + 1e-06) * gain_ref[...].astype(jnp.float32)).astype(
        jnp.bfloat16
    )
    rows = packed_ref.shape[0]
    tokens = normed.shape[0]
    at = lax.broadcasted_iota(jnp.int32, (rows, tokens), 0)
    pick = (at == row_ref[0:1, :]) | (at == row_ref[1:2, :])
    pick = pick.astype(jnp.float32).astype(jnp.bfloat16)
    packed_ref[...] = jnp.dot(pick, normed, preferred_element_type=jnp.float32).astype(jnp.bfloat16)


def norm_pack(near, left_up, right_down, gain, rows_t, weights):
    tokens, width = near.shape
    slots = 64 * CAP
    whole = pl.BlockSpec(memory_space=pltpu.VMEM)
    return pl.pallas_call(
        norm_pack_kernel,
        out_shape=(
            jax.ShapeDtypeStruct((tokens, width), jnp.bfloat16),
            jax.ShapeDtypeStruct((slots, width), jnp.bfloat16),
            jax.ShapeDtypeStruct(weights.shape, jnp.float32),
        ),
        in_specs=[whole] * 6,
        out_specs=(whole, whole, whole),
        compiler_params=pltpu.CompilerParams(vmem_limit_bytes=24 * MIB),
        name="norm_pack",
    )(near, left_up, right_down, gain, rows_t, weights)


def combine_kernel(back_ref, row_ref, weight_ref, out_ref):
    tokens, slots = out_ref.shape[0], back_ref.shape[0]
    at = lax.broadcasted_iota(jnp.int32, (tokens, slots), 1)
    back = back_ref[...]
    total = None
    for k in range(TOP):
        pick = (at == row_ref[:, k : k + 1]).astype(jnp.float32).astype(jnp.bfloat16)
        term = weight_ref[:, k : k + 1] * jnp.dot(pick, back, preferred_element_type=jnp.float32)
        total = term if total is None else total + term
    out_ref[...] = total.astype(jnp.bfloat16)


def combine(back, rows, weights):
    whole = pl.BlockSpec(memory_space=pltpu.VMEM)
    return pl.pallas_call(
        combine_kernel,
        out_shape=jax.ShapeDtypeStruct((rows.shape[0], back.shape[1]), jnp.bfloat16),
        in_specs=[whole] * 3,
        out_specs=whole,
        compiler_params=pltpu.CompilerParams(vmem_limit_bytes=24 * MIB),
        name="combine",
    )(back, rows, weights)


def expert_kernel(
    x_ref,
    gate_ref,
    up_hbm,
    down_hbm,
    gate2_hbm,
    up2_hbm,
    down2_hbm,
    out_ref,
    up_ref,
    gate2_ref,
    up2_ref,
    down_ref,
    act_ref,
    in_sem,
    down_sem,
):
    hidden_units = gate_ref.shape[1]
    width = x_ref.shape[1]
    step, wide = 256, 512
    per_half = hidden_units // step

    def own_copies(j):
        at = pl.ds(j * step, step)
        return (pltpu.make_async_copy(up_hbm.at[:, at], up_ref.at[:, at], in_sem.at[2, j]),)

    def first_copies(j):
        at = pl.ds(j * step, step)
        return (
            pltpu.make_async_copy(gate2_hbm.at[:, at], gate2_ref.at[:, at], in_sem.at[0, j]),
            pltpu.make_async_copy(up2_hbm.at[:, at], up2_ref.at[:, at], in_sem.at[1, j]),
        )

    def second_copies(j):
        at = pl.ds(j * wide, wide)
        return tuple(
            pltpu.make_async_copy(
                down.at[:, at],
                down_ref.at[pl.ds(half * hidden_units, hidden_units), at],
                down_sem.at[half, j],
            )
            for half, down in enumerate((down_hbm, down2_hbm))
        )

    loads = [own_copies(j) for j in range(per_half)]
    loads += [first_copies(j) for j in range(per_half)]
    loads += [second_copies(j) for j in range(width // wide)]
    ahead = 2
    for copies in loads[:ahead]:
        for copy in copies:
            copy.start()
    for j, copies in enumerate(loads):
        for copy in loads[j + ahead] if j + ahead < len(loads) else ():
            copy.start()
        if j >= per_half:
            for copy in copies:
                copy.wait()
        if j < 2 * per_half:
            gate, up = (gate_ref, up_ref) if j < per_half else (gate2_ref, up2_ref)
            at = slice((j % per_half) * step, (j % per_half + 1) * step)
            x = x_ref[...]
            gated = jnp.dot(x, gate[:, at], preferred_element_type=jnp.float32)
            if j < per_half:
                for copy in copies:
                    copy.wait()
            upward = jnp.dot(x, up[:, at], preferred_element_type=jnp.float32)
            act_ref[:, j * step : (j + 1) * step] = (
                gated / (1.0 + jnp.exp(-gated)) * upward
            ).astype(jnp.bfloat16)
        else:
            at = slice((j - 2 * per_half) * wide, (j - 2 * per_half + 1) * wide)
            out_ref[:, at] = jnp.dot(
                act_ref[...], down_ref[:, at], preferred_element_type=jnp.float32
            ).astype(jnp.bfloat16)


def whole_expert(rows, own, swapped):
    slots, width = rows.shape
    units = own[0].shape[1]
    anywhere = pl.BlockSpec(memory_space=pl.ANY)
    whole = pl.BlockSpec(memory_space=pltpu.VMEM)
    return pl.pallas_call(
        expert_kernel,
        out_shape=jax.ShapeDtypeStruct(rows.shape, jnp.bfloat16),
        in_specs=[whole] * 2 + [anywhere] * 5,
        out_specs=whole,
        scratch_shapes=[
            pltpu.VMEM((width, units), jnp.bfloat16),
            pltpu.VMEM((width, units), jnp.bfloat16),
            pltpu.VMEM((width, units), jnp.bfloat16),
            pltpu.VMEM((2 * units, width), jnp.bfloat16),
            pltpu.VMEM((slots, 2 * units), jnp.bfloat16),
            pltpu.SemaphoreType.DMA((3, 3)),
            pltpu.SemaphoreType.DMA((2, 8)),
        ],
        compiler_params=pltpu.CompilerParams(vmem_limit_bytes=EXPERT_MIB * MIB),
        name="whole_expert",
    )(rows, *own, *swapped)


def project_kernel(first, heads_ref, weight_ref, send_ref, keep_ref):
    wide = weight_ref.shape[2]
    half = send_ref.shape[0]
    heads = heads_ref[first : first + 2 * half, :]
    for piece in range(weight_ref.shape[0]):
        at = slice(piece * wide, (piece + 1) * wide)
        out = jnp.dot(heads, weight_ref[piece], preferred_element_type=jnp.float32).astype(
            jnp.bfloat16
        )
        send_ref[:, at] = out[:half]
        keep_ref[:, at] = out[half:]


def project(heads, weight, tokens, first):
    width = heads.shape[1]
    pieces, _, wide = weight.shape
    half = jax.ShapeDtypeStruct((tokens // 2, pieces * wide), jnp.bfloat16)
    whole = pl.BlockSpec(memory_space=pltpu.VMEM)
    return pl.pallas_call(
        functools.partial(project_kernel, first),
        out_shape=(half, half),
        in_specs=[whole, whole],
        out_specs=(whole, whole),
        compiler_params=pltpu.CompilerParams(vmem_limit_bytes=24 * MIB),
        cost_estimate=pl.CostEstimate(
            flops=1, bytes_accessed=2 * (width + tokens) * pieces * wide, transcendentals=0
        ),
        name="project",
    )(heads, weight)


def added(*terms):
    total = terms[0].astype(jnp.float32)
    for term in terms[1:]:
        total = total + term.astype(jnp.float32)
    return total.astype(jnp.bfloat16)


def reduce_over_experts(heads_out, wo_pieces):
    mid = D // 2

    def swapped(part):
        return lax.ppermute(part, "core", SWAP)

    def up(part):
        return lax.ppermute(part, "x", [(i, (i + 1) % 4) for i in range(4)])

    def down(part):
        return lax.ppermute(part, "x", [(i, (i - 1) % 4) for i in range(4)])

    far_send, far_keep = project(heads_out, wo_pieces, 2 * BLOCK, 4 * BLOCK)
    far_swap = swapped(far_send)
    far_left, far_right, heads_out = lax.optimization_barrier(
        (
            added(far_keep[:, :mid], far_swap[:, :mid]),
            added(far_keep[:, mid:], far_swap[:, mid:]),
            heads_out,
        )
    )
    far_up, far_down = up(far_left), down(far_right)
    next_send, next_keep = project(heads_out, wo_pieces, 4 * BLOCK, 0)
    next_send, heads_out = lax.optimization_barrier((next_send, heads_out))
    next_swap = swapped(next_send)
    right_up = up(added(next_keep[:BLOCK, mid:], next_swap[:BLOCK, mid:]))
    left_down = down(added(next_keep[BLOCK:, :mid], next_swap[BLOCK:, :mid]))
    own_send, own_keep = project(heads_out, wo_pieces, 2 * BLOCK, 6 * BLOCK)
    own_swap = swapped(own_send)
    far_up, far_down, next_keep, next_swap = lax.optimization_barrier(
        (far_up, far_down, next_keep, next_swap)
    )
    left_up = up(added(next_keep[:BLOCK, :mid], next_swap[:BLOCK, :mid], far_up))
    right_down = down(added(next_keep[BLOCK:, mid:], next_swap[BLOCK:, mid:], far_down))
    return own_keep, own_swap, left_up, right_up, left_down, right_down


def slots_of(routes):
    tok_dev = routes.shape[0]
    flat_routes = routes.reshape(-1)
    matched = (flat_routes[:, None] == jnp.arange(64, dtype=jnp.int32)[None, :]).astype(jnp.int32)
    slot_index = jnp.sum((jnp.cumsum(matched, axis=0) - matched) * matched, axis=1)
    return (flat_routes * CAP + slot_index).reshape(tok_dev, TOP)


def local(
    hidden,
    query,
    candidate_key_value,
    prefix_key_value,
    segment_ids,
    o_weight,
    norm_gain,
    routes,
    route_weights,
    w_gate,
    w_up,
    w_down,
):
    heads_dev = query.shape[1] // HEAD_SIZE
    expert_index = lax.axis_index("x") * 2 + lax.axis_index("core")
    head = (expert_index * heads_dev) // (QUERY_HEADS // KEY_VALUE_HEADS)

    def of_head(key_value):
        part = lax.dynamic_slice_in_dim(key_value, head * HEAD_SIZE, HEAD_SIZE, 2)
        return part.reshape(key_value.shape[0], 2 * HEAD_SIZE)

    own_prefix = of_head(prefix_key_value)
    n_list = lax.axis_size(LIST)
    prefix = lax.all_to_all(
        jnp.broadcast_to(own_prefix[None], (n_list,) + own_prefix.shape),
        LIST,
        split_axis=0,
        concat_axis=0,
        tiled=True,
    ).reshape(-1, 2 * HEAD_SIZE)
    wo_pieces = lax.all_gather(o_weight, LIST, axis=0, tiled=False)
    at, core = lax.axis_index("x"), lax.axis_index("core")

    def block_of(step, own):
        return 2 * ((at + step) % 4) + (core if own else 1 - core)

    order = jnp.stack(
        [
            block_of(step, own)
            for step, own in (
                (1, False),
                (3, False),
                (1, True),
                (3, True),
                (2, False),
                (2, True),
                (0, False),
                (0, True),
            )
        ]
    ).astype(jnp.int32)
    heads_out = attention(query, prefix, of_head(candidate_key_value), segment_ids[0], order)
    own = (w_gate[0], w_up[0], w_down[0])
    swapped = tuple(lax.ppermute(w, "core", SWAP) for w in own)
    rows = slots_of(routes)
    heads_out, swapped, rows, rows_t, gain = lax.optimization_barrier(
        (heads_out, swapped, rows, rows.T, norm_gain.reshape(1, D))
    )
    parts = reduce_over_experts(heads_out, wo_pieces)
    own_keep, own_swap, left_up, right_up, left_down, right_down = parts
    near = near_sum(hidden, own_keep, own_swap, left_down, right_up)
    attended, packed, weights = norm_pack(
        near, left_up, right_down, gain, rows_t, route_weights
    )

    def across(slots):
        return lax.all_to_all(
            slots.reshape(64, CAP, D), CHIP, split_axis=0, concat_axis=0, tiled=True
        ).reshape(64 * CAP, D)

    back = across(whole_expert(across(packed), own, swapped))
    return attended, combine(back, rows, weights)


def solution(mesh):
    fine = Mesh(mesh.devices.reshape(4, 4, 4, 2), ALL)
    placed = (
        P(ALL, None),
        P(LIST, EXPERT),
        P(LIST, None, None),
        P(LIST, None, None),
        P(LIST, None),
        P(EXPERT, LIST),
        P(),
        P(ALL, None),
        P(ALL, None),
        P(ALL, None, None),
        P(ALL, None, None),
        P(ALL, None, None),
    )
    return jax.shard_map(
        local,
        mesh=fine,
        in_specs=placed,
        out_specs=(P(ALL, None), P(ALL, None)),
        check_vma=False,
    )
```
